256 devices in a mesh: grp: 2 (over z_lo), dp: 32 (over z_hi, y, core), mp: 4 (over x).
Axes of the slice: x: 4, y: 4, z: 8 (z_hi: 4, z_lo: 2; z = z_hi * 2 + z_lo), core: 2. Of those that a mesh axis runs over, the one named last changes fastest.
Arguments:
- states: bfloat16 [2, 16384, 1024], P('grp', 'dp')
- w_in: bfloat16 [1024, 4096], P(('grp', 'dp'), 'mp'), may hold values from -0.1875 to 0.1875
- b_in: float32 [4096], P('mp'), may hold values from -3 to 3
- w_out: bfloat16 [4096, 1024], P('mp', ('grp', 'dp')), may hold values from -0.09375 to 0.09375
- b_out: float32 [1024], replicated, may hold values from -3 to 3
- ln_gain: float32 [1024], replicated, may hold values from 0.25 to 1.75
- ln_bias: float32 [1024], replicated, may hold values from -2 to 2
- lengths: int32 [4096], P('dp'), may hold values from 128 to 512, as said below
- neg_ids: int32 [256, 32], P('dp'), may hold values from 0 to 4095, as said below
- neg_count: int32 [256], P('dp'), may hold values from 8 to 32
- pos_ids: int32 [256], P('dp'), may hold values from 0 to 4095
Outputs:
- encoded: bfloat16 [2, 16384, 1024], P('grp', 'dp', 'mp')
- question_direction_derivative: float32 [256, 1024], P('dp', 'mp')
- query_loss: float32 [256], P('dp')
The draws below stay inside these ranges and needn't reach their ends.
Inputs may be any that keep to these rules, and one draw needn't show every extreme that they name: `lengths`: each is 128, 256 or 512. `neg_ids`: for each query its 32 entries and its positive are distinct passage numbers; entries at or after the query's neg_count are ignored.
All inputs are finite; a program needn't handle non-finite values.
Results may differ from the reference program's by a relative error of at most 0.0054.
Values may be sent and summed in bfloat16 or wider, within the bound.
No kernel may reach another device: no remote copies, remote signals or barrier semaphores. Data moves between devices by JAX's collectives and lax.ppermute only.
A program may use at most 64 MiB of HBM per device.

```python
import jax
import jax.numpy as jnp
from jax import lax

EMBED_DIMENSION = 1024
FF = 4096
WIN = 4
QLEN = 64
NEG_MAX = 32
PASS_DEV = 128
ROWS_DEV = 512
PASSAGES = 4096
QUERIES = 256
ROWS = 16384
N_DP = 32


def draw_states(key, part):
    key = jax.random.fold_in(key, 11)
    keys = jax.random.split(key, 4)
    common_pass = jax.random.normal(keys[0], (PASSAGES, 1, EMBED_DIMENSION), jnp.float32)
    common_query = jax.random.normal(keys[1], (QUERIES, 1, EMBED_DIMENSION), jnp.float32)
    noise_pass = jax.random.normal(keys[2], (PASSAGES, WIN, EMBED_DIMENSION), jnp.float32)
    noise_query = jax.random.normal(keys[3], (QUERIES, QLEN, EMBED_DIMENSION), jnp.float32)
    first = ((common_pass + noise_pass) * 0.7).reshape(ROWS, EMBED_DIMENSION)
    second = ((common_query + noise_query) * 0.7).reshape(ROWS, EMBED_DIMENSION)
    return jnp.stack([second, first]).astype(jnp.bfloat16)


def draw_lengths(key, part):
    key = jax.random.fold_in(key, 12)
    choice_index = jax.random.randint(key, (PASSAGES,), 0, 3)
    table = jnp.array([128, 256, 512], jnp.int32)
    return table[choice_index]


def candidate_ids(key):
    keys = jax.random.split(key, 4)
    order = jax.random.permutation(keys[0], N_DP)
    first = jax.random.randint(keys[1], (QUERIES, NEG_MAX + 1), 0, N_DP)
    second = jax.random.randint(keys[2], (QUERIES, NEG_MAX + 1), 0, N_DP)
    shard = order[jnp.minimum(first, second)]
    base = jax.random.randint(keys[3], (QUERIES, 1), 0, PASS_DEV)
    local_ids = (base + jnp.arange(NEG_MAX + 1, dtype=jnp.int32)[None, :]) % PASS_DEV
    return (shard * PASS_DEV + local_ids).astype(jnp.int32)


def draw_neg_ids(key, part):
    picked = candidate_ids(key)
    return picked[:, 1:]


def draw_pos_ids(key, part):
    picked = candidate_ids(key)
    return picked[:, 0]


def touch_ends(entries, own_key, low, largest):
    longest = entries.shape.index(max(entries.shape))
    spots = []
    for shift in (0, 1):
        where = [jax.random.randint(jax.random.fold_in(own_key, axis), (), 0, length) for axis, length in enumerate(entries.shape)]
        where[longest] = (where[longest] + shift) % entries.shape[longest]
        spots.append(tuple(where))
    return entries.at[spots[0]].set(low).at[spots[1]].set(largest)


def steps_of(stream_key, extent, pieces, low, top_value):
    level, own = 1.0, jax.random.fold_in(stream_key, 6)
    for axis_at, parts in pieces:
        steps = jnp.exp(jax.random.uniform(jax.random.fold_in(own, axis_at), (parts,), jnp.float32, low / len(pieces), top_value / len(pieces)))
        level = level * jnp.repeat(steps, extent[axis_at] // parts).reshape([-1 if axis == axis_at else 1 for axis in range(len(extent))])
    return level


def gaussian(rng, shape, width, most, shards=(), held_as=jnp.bfloat16):
    drawn = jax.random.normal(rng, shape, jnp.float32) * width
    if len(shards) > 0:
        drawn = steps_of(rng, shape, shards, -0.22, 0.18) * drawn
    return jnp.clip(drawn, min=-most, max=most).astype(held_as)


def setup_inputs(seed: int = 0) -> dict:
    splits = jax.random.split(jax.random.key(seed), 12)
    states = draw_states(jax.random.fold_in(splits[11], 71), 0)
    w_in = gaussian(splits[1], (EMBED_DIMENSION, FF), EMBED_DIMENSION ** -0.5, 0.1875, ((0, 64), (1, 4)))
    b_in = gaussian(splits[2], (FF,), 0.5, 3.0, ((0, 4),), jnp.float32)
    w_out = gaussian(splits[3], (FF, EMBED_DIMENSION), FF ** -0.5, 0.09375, ((0, 4), (1, 64)))
    b_out = gaussian(splits[4], (EMBED_DIMENSION,), 0.5, 3.0, (), jnp.float32)
    ln_gain = jnp.clip(1.0 + 0.15 * jax.random.normal(splits[5], (EMBED_DIMENSION,), jnp.float32), 0.25, 1.75)
    ln_bias = gaussian(splits[6], (EMBED_DIMENSION,), 0.3, 2.0, (), jnp.float32)
    lengths = draw_lengths(jax.random.fold_in(splits[11], 71), 0)
    neg_ids = draw_neg_ids(jax.random.fold_in(splits[11], 71), 0)
    neg_count = touch_ends(jax.random.randint(splits[9], (QUERIES,), NEG_MAX // 4, NEG_MAX + 1), jax.random.fold_in(splits[9], 1), NEG_MAX // 4, NEG_MAX).astype(jnp.int32)
    pos_ids = draw_pos_ids(jax.random.fold_in(splits[11], 71), 0)
    return dict(states=states, w_in=w_in, b_in=b_in, w_out=w_out, b_out=b_out, ln_gain=ln_gain, ln_bias=ln_bias, lengths=lengths, neg_ids=neg_ids, neg_count=neg_count, pos_ids=pos_ids)


sharpness_divisor = 0.05
window_tokens = 128
eps_norm = 1e-05
eps_unit = 1e-06

def encode(block_rows, w_in, b_in, w_out, b_out, ln_gain, ln_bias):
    pre = jnp.dot(block_rows, w_in, preferred_element_type=jnp.float32) + b_in
    hidden = jax.nn.gelu(pre, approximate=False).astype(jnp.bfloat16)
    mixed_sum = jnp.dot(hidden, w_out, preferred_element_type=jnp.float32)
    summed = block_rows.astype(jnp.float32) + mixed_sum + b_out
    center = lax.optimization_barrier(jnp.mean(summed, axis=1, keepdims=True))
    spread = lax.optimization_barrier(jnp.mean(jnp.square(summed - center), axis=1, keepdims=True))
    normed = (summed - center) * lax.rsqrt(spread + eps_norm)
    return (normed * ln_gain + ln_bias).astype(jnp.bfloat16)

def reference(states, w_in, b_in, w_out, b_out, ln_gain, ln_bias, lengths, neg_ids, neg_count, pos_ids):
    blocks = states.reshape(2 * N_DP, ROWS_DEV, EMBED_DIMENSION)
    encoded = lax.map(lambda block_rows: encode(block_rows, w_in, b_in, w_out, b_out, ln_gain, ln_bias), blocks)
    encoded = encoded.reshape(2, ROWS, EMBED_DIMENSION)
    encoded_f = encoded.astype(jnp.float32)
    windows = encoded_f[1].reshape(PASSAGES, WIN, EMBED_DIMENSION)
    live_mask = (jnp.arange(WIN)[None, :] * window_tokens < lengths[:, None]).astype(jnp.float32)
    passage_emb = (lax.optimization_barrier(jnp.sum(windows * live_mask[:, :, None], axis=1)) / lax.optimization_barrier(jnp.sum(live_mask, axis=1, keepdims=True))).astype(jnp.bfloat16)
    query_emb = lax.optimization_barrier(jnp.mean(encoded_f[0].reshape(QUERIES, QLEN, EMBED_DIMENSION), axis=1)).astype(jnp.bfloat16)
    angle_similarity_scores = lax.dot_general(query_emb, passage_emb, (((1,), (1,)), ((), ())), preferred_element_type=jnp.float32)
    query_sq = lax.optimization_barrier(jnp.sum(jnp.square(query_emb.astype(jnp.float32)), axis=1))
    passage_sq = lax.optimization_barrier(jnp.sum(jnp.square(passage_emb.astype(jnp.float32)), axis=1))
    question_reciprocal_length = jnp.sqrt(query_sq / EMBED_DIMENSION + eps_unit)
    document_reciprocal_length = jnp.sqrt(passage_sq / EMBED_DIMENSION + eps_unit)
    sharpened_similarity_scores = angle_similarity_scores / (EMBED_DIMENSION * sharpness_divisor * question_reciprocal_length[:, None] * document_reciprocal_length[None, :])
    slot_ids = jnp.arange(NEG_MAX)
    usable = (slot_ids[None, :] < neg_count[:, None]).astype(jnp.float32)
    rows_index = jnp.broadcast_to(jnp.arange(QUERIES)[:, None], neg_ids.shape)
    members = jnp.zeros((QUERIES, PASSAGES), jnp.float32).at[rows_index, neg_ids].add(usable)
    matching_document = (pos_ids[:, None] == jnp.arange(PASSAGES)[None, :]).astype(jnp.float32)
    candidate_probabilities = jnp.exp(sharpened_similarity_scores) * (members + matching_document)
    line_aggregates = lax.optimization_barrier(jnp.sum(candidate_probabilities, axis=1))
    pos_score = lax.optimization_barrier(jnp.sum(sharpened_similarity_scores * matching_document, axis=1))
    query_loss = jnp.log(line_aggregates) - pos_score
    length_one_vectors = passage_emb.astype(jnp.float32) / (jnp.sqrt(jnp.float32(EMBED_DIMENSION)) * document_reciprocal_length)[:, None]
    question_direction_derivative = jnp.dot(candidate_probabilities / line_aggregates[:, None] - matching_document, length_one_vectors, precision=lax.Precision.HIGHEST, preferred_element_type=jnp.float32) / sharpness_divisor
    return (encoded, question_direction_derivative, query_loss)
```

```python
import functools

import jax
import jax.numpy as jnp
import numpy as np
from jax import lax
from jax.experimental import pallas as pl
from jax.experimental.pallas import tpu as pltpu
from jax.sharding import Mesh, PartitionSpec as P

WIN = 4
QLEN = 64
WINDOW_TOKENS = 128
SHARPNESS = 0.05
EPS_NORM = 1e-05
EPS_UNIT = 1e-06

N_GRP, N_ZH, N_Y, N_C, N_MP = 2, 4, 4, 2, 4
N_Z = N_GRP * N_ZH
BF = jnp.bfloat16
F32 = jnp.float32
VMEM = pl.BlockSpec(memory_space=pltpu.VMEM)
SMEM = pl.BlockSpec(memory_space=pltpu.SMEM)
ANY = pl.BlockSpec(memory_space=pl.ANY)
NT = (((1,), (1,)), ((), ()))


def params():
    return pltpu.CompilerParams(vmem_limit_bytes=40 * 1024 * 1024)


def cost(flops, size):
    return pl.CostEstimate(flops=flops, bytes_accessed=size, transcendentals=0)


def shift(block, axis, distance):
    n = lax.axis_size(axis)
    return lax.ppermute(block, axis, [(i, (i + distance) % n) for i in range(n)])


def shift_refresh(block, axis, distance):
    n = lax.axis_size(axis)
    route = [(n + i, n + (i + distance) % n) for i in range(n)]
    return lax.ppermute(block, ("grp", axis), route)


def spread(block, axes, n):
    filled = jnp.broadcast_to(block[None], (n,) + block.shape)
    return lax.all_to_all(filled, axes, 0, 0, tiled=True)


def assemble(place, sources, weights, sems):
    y, c = place[1], place[2]
    copies = []
    for other in range(N_C):
        core = c if other == 0 else 1 - c
        for k in range(N_Y):
            line = lax.rem(y - k + N_Y, N_Y)
            copies.append(
                pltpu.make_async_copy(
                    sources[other * N_Y + k],
                    weights.at[:, line * N_C + core],
                    sems.at[other * N_Y + k],
                )
            )
    for copy in copies:
        copy.start()
    for copy in copies:
        copy.wait()


def hidden_kernel(place, x_ref, b_ref, *rest):
    sources, (h_ref, weights, sems) = rest[:8], rest[8:]
    assemble(place, sources, weights, sems)
    depth = x_ref.shape[1]
    width = h_ref.shape[1]
    tile = 256
    for t in range(width // tile):
        cols = slice(t * tile, (t + 1) * tile)
        w = weights[:, :, :, cols].reshape(depth, tile)
        pre = jnp.dot(x_ref[...], w, preferred_element_type=F32) + b_ref[:, cols]
        h_ref[:, cols] = (0.5 * pre * (1.0 + lax.erf(pre * np.float32(0.5**0.5)))).astype(BF)


def partial_kernel(place, h_ref, *rest):
    sources, (own_ref, s1, s2, s3, weights, total, sems) = rest[:8], rest[8:]
    assemble(place, sources, weights, sems)
    m = place[3]
    width = weights.shape[-1]
    tile = 256
    planes = tile // 128
    for t in range(total.shape[1] // tile):
        w = weights[t * planes : (t + 1) * planes].reshape(tile, width)
        total[:, t * tile : (t + 1) * tile] = lax.dot_general(
            h_ref[...], w, NT, preferred_element_type=F32
        )
    rows = own_ref.shape[0]
    for k, out in ((0, own_ref), (1, s1), (2, s2), (3, s3)):
        j = lax.rem(m + k, N_MP)
        out[...] = total[pl.ds(pl.multiple_of(j * rows, rows), rows), :].astype(out.dtype)


def norm_kernel(place, own, r1, r2, r3, x_ref, b_out, gain, bias, lens, e0, e1, e2, e3, p_ref, q_ref, enc):
    m = place[3]
    rows, width = own.shape
    x = x_ref[pl.ds(pl.multiple_of(m * rows, rows), rows), :]
    summed = own[...] + r1[...].astype(F32) + r2[...].astype(F32) + r3[...].astype(F32)
    summed = x.astype(F32) + summed + b_out[...]
    center = jnp.mean(summed, axis=1, keepdims=True)
    off = summed - center
    spread_ = jnp.mean(off * off, axis=1, keepdims=True)
    coded = (off * lax.rsqrt(spread_ + EPS_NORM) * gain[...] + bias[...]).astype(BF)
    enc[...] = coded
    part = width // N_MP
    for k, out in ((0, e0), (1, e1), (2, e2), (3, e3)):
        j = lax.rem(m + k, N_MP)
        out[...] = enc[:, pl.ds(pl.multiple_of(j * part, part), part)]
    n_pass = p_ref.shape[0]
    lens_m = lens[pl.ds(pl.multiple_of(m * n_pass, n_pass), n_pass), :]
    row = lax.broadcasted_iota(jnp.int32, (n_pass, rows), 1)
    slab = lax.broadcasted_iota(jnp.int32, (n_pass, rows), 0)
    alive = (row // WIN == slab) & ((row % WIN) * WINDOW_TOKENS < lens_m)
    live = jnp.where(alive, 1.0, 0.0).astype(F32)
    count = jnp.sum(live, axis=1, keepdims=True)
    p_ref[...] = (jnp.dot(live.astype(BF), coded, preferred_element_type=F32) / count).astype(BF)
    n_q = q_ref.shape[0]
    rowq = lax.broadcasted_iota(jnp.int32, (16, rows), 1)
    slabq = lax.broadcasted_iota(jnp.int32, (16, rows), 0)
    pick = jnp.where(rowq // QLEN == slabq, 1.0, 0.0).astype(BF)
    qs = jnp.dot(pick, coded, preferred_element_type=F32) * (1.0 / QLEN)
    q_ref[...] = qs[:n_q].astype(BF)


def pieces(v):
    a = v.astype(BF)
    rest = v - a.astype(F32)
    b = rest.astype(BF)
    return a, b, (rest - b.astype(F32)).astype(BF)


def score_kernel(place, q_ref, ids, p0, p1, p2, p3, out):
    zh, y, c, m = place[0], place[1], place[2], place[3]
    blocks = (p0, p1, p2, p3)
    size, width = p0.shape
    n_q = q_ref.shape[0]
    each = size // N_ZH
    n_slots = 32
    q = q_ref[...]
    qf = q.astype(F32)
    a = jnp.sqrt(jnp.sum(qf * qf, axis=1, keepdims=True) / width + EPS_UNIT)
    ones = jnp.ones((16, width), BF)
    lane = lax.broadcasted_iota(jnp.int32, (1, size), 1)
    zh_of = lax.rem(zh - lane // each + N_ZH, N_ZH)
    neg = ids[:, :n_slots]
    count = ids[:, n_slots : n_slots + 1]
    pos = ids[:, n_slots + 1 : n_slots + 2]
    total = jnp.zeros((n_q, 1), F32)
    score_pos = jnp.zeros((n_q, 1), F32)
    grads = jnp.zeros((6 * n_q, width), F32)
    for k, block in enumerate(blocks):
        p = block[...]
        pf = p.astype(F32)
        sq = pf * pf
        hi = sq.astype(BF)
        lo = (sq - hi.astype(F32)).astype(BF)
        b2 = lax.dot_general(ones, hi, NT, preferred_element_type=F32)
        b2 = b2 + lax.dot_general(ones, lo, NT, preferred_element_type=F32)
        b = jnp.sqrt(b2[:1] / width + EPS_UNIT)
        dots = lax.dot_general(q, p, NT, preferred_element_type=F32)
        s = dots / (width * SHARPNESS * a * b)
        line = lax.rem(y - k + N_Y, N_Y)
        number = ((zh_of * N_Y + line) * N_C + c) * (each * N_MP) + m * each + lax.rem(lane, each)
        match = jnp.where(pos == number, 1.0, 0.0).astype(F32)
        cand = match
        for j in range(n_slots):
            hit = (neg[:, j : j + 1] == number) & (j < count)
            cand = cand + jnp.where(hit, 1.0, 0.0)
        w = jnp.exp(s) * cand
        total = total + jnp.sum(w, axis=1, keepdims=True)
        score_pos = score_pos + jnp.sum(s * match, axis=1, keepdims=True)
        unit = 1.0 / (np.float32(width**0.5) * b)
        coef = jnp.concatenate(pieces(w * unit) + pieces(match * unit), axis=0)
        grads = grads + jnp.dot(coef, p, preferred_element_type=F32)
    pull = grads[:n_q] + grads[n_q : 2 * n_q] + grads[2 * n_q : 3 * n_q]
    toward = grads[3 * n_q : 4 * n_q] + grads[4 * n_q : 5 * n_q] + grads[5 * n_q :]
    part = width // N_MP
    own = n_q // N_C
    half = part // 2
    stats = jnp.concatenate(
        [jnp.broadcast_to(total, (n_q, half)), jnp.broadcast_to(score_pos, (n_q, half))], axis=1
    )
    for g in range(N_GRP):
        for cc in range(N_C):
            rows = slice(cc * own, (cc + 1) * own)
            for mm in range(N_MP):
                cols = slice(mm * part, (mm + 1) * part)
                d = (g * N_C + cc) * N_MP + mm
                out[d, 0:own, :] = pull[rows, cols]
                out[d, own : 2 * own, :] = toward[rows, cols]
                out[d, 2 * own : 3 * own, :] = stats[rows]


def final_kernel(arrived, grad, loss):
    peers = arrived.shape[0] // N_GRP
    own, part = grad.shape
    acc = arrived[peers]
    for d in range(peers + 1, 2 * peers):
        acc = acc + arrived[d]
    total = acc[2 * own :, :1]
    score = acc[2 * own :, part // 2 : part // 2 + 1]
    grad[...] = (acc[:own] / total - acc[own : 2 * own]) / SHARPNESS
    loss[...] = jnp.broadcast_to(jnp.log(total) - score, loss.shape)


def body(states, w_in, b_in, w_out, b_out, ln_gain, ln_bias, lengths, neg_ids, neg_count, pos_ids):
    x = states[0]
    rows, width = x.shape
    hid = b_in.shape[0]
    shard = w_in.shape[0]
    place = jnp.stack([lax.axis_index(a) for a in ("zh", "y", "c", "mp")]).astype(jnp.int32)

    packed = jnp.concatenate([neg_ids, neg_count[:, None], pos_ids[:, None]], axis=1)
    other_packed = shift(packed, "c", 1)
    first = lax.axis_index("c") == 0
    ids = jnp.concatenate(
        [jnp.where(first, packed, other_packed), jnp.where(first, other_packed, packed)], axis=0
    )

    both = jnp.concatenate([w_in, w_out.T], axis=0)
    along_z = spread(both, ("grp", "zh"), N_Z)
    z_in, z_out = along_z[:, :shard], along_z[:, shard:]
    lines_in = [z_in] + [shift(z_in, "y", k) for k in (1, 2, 3)]
    lines_out = [z_out] + [shift(z_out, "y", k) for k in (1, 2, 3)]
    lines_in = lines_in + [shift(v, "c", 1) for v in lines_in]
    lines_out = lines_out + [shift(v, "c", 1) for v in lines_out]
    weight_scratch = [
        pltpu.VMEM((N_Z, N_Y * N_C, shard, hid), BF),
        pltpu.SemaphoreType.DMA((8,)),
    ]
    hidden = pl.pallas_call(
        hidden_kernel,
        out_shape=jax.ShapeDtypeStruct((rows, hid), BF),
        in_specs=[SMEM, VMEM, VMEM] + [ANY] * 8,
        out_specs=VMEM,
        scratch_shapes=weight_scratch,
        compiler_params=params(),
        cost_estimate=cost(2 * rows * width * hid * 3, 4 << 20),
        name="hidden",
    )(place, x, b_in[None], *lines_in)

    part_rows = rows // N_MP
    own, s1, s2, s3 = pl.pallas_call(
        partial_kernel,
        out_shape=[jax.ShapeDtypeStruct((part_rows, width), F32)]
        + [jax.ShapeDtypeStruct((part_rows, width), BF)] * 3,
        in_specs=[SMEM, VMEM] + [ANY] * 8,
        out_specs=[VMEM] * 4,
        scratch_shapes=[weight_scratch[0], pltpu.VMEM((rows, width), F32), weight_scratch[1]],
        compiler_params=params(),
        cost_estimate=cost(2 * rows * width * hid, 4 << 20),
        name="partial",
    )(place, hidden, *lines_out)
    r2, r1, r3 = shift(s2, "mp", 2), shift(s1, "mp", 1), shift(s3, "mp", 3)

    part = width // N_MP
    n_pass = part_rows // WIN
    n_own_q = part_rows // QLEN
    *enc, passages, queries = pl.pallas_call(
        norm_kernel,
        out_shape=[jax.ShapeDtypeStruct((part_rows, part), BF)] * 4
        + [
            jax.ShapeDtypeStruct((n_pass, width), BF),
            jax.ShapeDtypeStruct((n_own_q, width), BF),
        ],
        in_specs=[SMEM] + [VMEM] * 9,
        out_specs=[VMEM] * 6,
        scratch_shapes=[pltpu.VMEM((part_rows, width), BF)],
        compiler_params=params(),
        cost_estimate=cost(2 * part_rows * width * 64, 3 << 20),
        name="norm",
    )(place, own, r1, r2, r3, x, b_out[None], ln_gain[None], ln_bias[None], lengths[:, None])

    along_zh = jnp.concatenate(
        [passages] + [shift_refresh(passages, "zh", k) for k in (1, 2, 3)], axis=0
    )
    lines = [along_zh] + [shift_refresh(along_zh, "y", k) for k in (1, 2, 3)]
    arrived_q = spread(queries, ("grp", "c", "mp"), N_GRP * N_C * N_MP)
    q_all = arrived_q[: N_C * N_MP].reshape(N_C * N_MP * n_own_q, width)

    own_q = n_own_q * N_MP
    peers = N_GRP * N_C * N_MP
    shares = pl.pallas_call(
        score_kernel,
        out_shape=jax.ShapeDtypeStruct((peers, 3 * own_q, part), F32),
        in_specs=[SMEM] + [VMEM] * 6,
        out_specs=VMEM,
        compiler_params=params(),
        cost_estimate=cost(2 * 512 * width * 200, 3 << 20),
        name="score",
    )(place, q_all, ids, *lines)
    arrived = lax.all_to_all(shares, ("grp", "c", "mp"), 0, 0, tiled=True)
    grad, loss = pl.pallas_call(
        final_kernel,
        out_shape=[
            jax.ShapeDtypeStruct((own_q, part), F32),
            jax.ShapeDtypeStruct((own_q, 128), F32),
        ],
        in_specs=[VMEM],
        out_specs=[VMEM] * 2,
        compiler_params=params(),
        name="final",
    )(arrived)

    m = lax.axis_index("mp")
    placed = [enc[0]] + [shift(enc[k], "mp", k) for k in (1, 2, 3)]
    encoded = jnp.zeros((N_MP, part_rows, part), BF)
    for k in range(N_MP):
        encoded = lax.dynamic_update_slice_in_dim(encoded, placed[k][None], (m - k) % N_MP, 0)
    return encoded.reshape(1, rows, part), grad, loss[:, 0]


def solution(mesh):
    fine = Mesh(
        mesh.devices.reshape(N_GRP, N_ZH, N_Y, N_C, N_MP), ("grp", "zh", "y", "c", "mp")
    )
    dp = ("zh", "y", "c")
    placed = (
        P("grp", dp, None),
        P(("grp",) + dp, "mp"),
        P("mp"),
        P("mp", ("grp",) + dp),
        P(),
        P(),
        P(),
        P(dp),
        P(dp, None),
        P(dp),
        P(dp),
    )
    return jax.shard_map(
        body,
        mesh=fine,
        in_specs=placed,
        out_specs=(P("grp", dp, "mp"), P(dp, "mp"), P(dp)),
        check_vma=False,
    )
```

```python
import jax
import jax.numpy as jnp
import numpy as np
from jax import lax
from jax.experimental import pallas as pl
from jax.experimental.pallas import tpu as pltpu
from jax.sharding import Mesh, PartitionSpec as P

WIN = 4
QLEN = 64
WINDOW_TOKENS = 128
SHARPNESS = 0.05
EPS_NORM = 1e-05
EPS_UNIT = 1e-06

N_GRP, N_ZH, N_Y, N_C, N_MP = 2, 4, 4, 2, 4
N_Z = N_GRP * N_ZH
BF = jnp.bfloat16
F32 = jnp.float32
VMEM = pl.BlockSpec(memory_space=pltpu.VMEM)
SMEM = pl.BlockSpec(memory_space=pltpu.SMEM)
ANY = pl.BlockSpec(memory_space=pl.ANY)
NT = (((1,), (1,)), ((), ()))
N_NEG = 32
DIGIT = 64


def params():
    return pltpu.CompilerParams(vmem_limit_bytes=40 * 1024 * 1024)


def cost(flops, size):
    return pl.CostEstimate(flops=flops, bytes_accessed=size, transcendentals=0)


def shift(block, axis, distance):
    n = lax.axis_size(axis)
    return lax.ppermute(block, axis, [(i, (i + distance) % n) for i in range(n)])


def shift_refresh(block, axis, distance):
    n = lax.axis_size(axis)
    route = [(n + i, n + (i + distance) % n) for i in range(n)]
    return lax.ppermute(block, ("grp", axis), route)


def spread(block, axes, n):
    filled = jnp.broadcast_to(block[None], (n,) + block.shape)
    return lax.all_to_all(filled, axes, 0, 0, tiled=True)


def ffn_kernel(place, x_ref, b_ref, *rest):
    firsts, seconds = rest[:8], rest[8:10]
    own_ref, s1, s2, s3, w1, w2, hidden, total, sems = rest[10:]
    y, c, m = place[1], place[2], place[3]
    hid = hidden.shape[1]
    half = seconds[0].shape[-1]
    early, late = [], []
    for other in range(N_C):
        core = c if other == 0 else 1 - c
        for k in range(N_Y):
            slot = lax.rem(y - k + N_Y, N_Y) * N_C + core
            first, second = firsts[other * N_Y + k], seconds[other]
            i = 3 * (other * N_Y + k)
            early.append(
                pltpu.make_async_copy(first.at[:, :, 0:hid], w1.at[:, slot], sems.at[i])
            )
            late.append(
                pltpu.make_async_copy(
                    first.at[:, :, hid : hid + half], w2.at[:, slot, :, 0:half], sems.at[i + 1]
                )
            )
            late.append(
                pltpu.make_async_copy(
                    second.at[:, k], w2.at[:, slot, :, half : 2 * half], sems.at[i + 2]
                )
            )
    for copy in early + late:
        copy.start()
    for copy in early:
        copy.wait()
    depth = x_ref.shape[1]
    tile = 256
    for t in range(hid // tile):
        cols = slice(t * tile, (t + 1) * tile)
        w = w1[:, :, :, cols].reshape(depth, tile)
        pre = jnp.dot(x_ref[...], w, preferred_element_type=F32) + b_ref[:, cols]
        hidden[:, cols] = (0.5 * pre * (1.0 + lax.erf(pre * np.float32(0.5**0.5)))).astype(BF)
    for copy in late:
        copy.wait()
    planes = tile // (w2.shape[1] * w2.shape[2])
    for t in range(total.shape[1] // tile):
        w = w2[t * planes : (t + 1) * planes].reshape(tile, hid)
        total[:, t * tile : (t + 1) * tile] = lax.dot_general(
            hidden[...], w, NT, preferred_element_type=F32
        )
    rows = own_ref.shape[0]
    for k, out in ((2, s2), (1, s1), (3, s3), (0, own_ref)):
        j = lax.rem(m + k, N_MP)
        out[...] = total[pl.ds(pl.multiple_of(j * rows, rows), rows), :].astype(out.dtype)


def norm_kernel(place, own, r1, r2, r3, x_ref, b_out, gain, bias, lens, lists, e0, e1, e2, e3, p_ref, q_ref, enc):
    m = place[3]
    rows, width = own.shape
    x = x_ref[pl.ds(pl.multiple_of(m * rows, rows), rows), :]
    summed = own[...] + r1[...].astype(F32) + r2[...].astype(F32) + r3[...].astype(F32)
    summed = x.astype(F32) + summed + b_out[...]
    center = jnp.mean(summed, axis=1, keepdims=True)
    off = summed - center
    spread_ = jnp.mean(off * off, axis=1, keepdims=True)
    coded = (off * lax.rsqrt(spread_ + EPS_NORM) * gain[...] + bias[...]).astype(BF)
    enc[...] = coded
    part = width // N_MP
    for k, out in ((0, e0), (1, e1), (2, e2), (3, e3)):
        j = lax.rem(m + k, N_MP)
        out[...] = enc[:, pl.ds(pl.multiple_of(j * part, part), part)]
    n_pass = p_ref.shape[0]
    lens_m = lens[pl.ds(pl.multiple_of(m * n_pass, n_pass), n_pass), :]
    row = lax.broadcasted_iota(jnp.int32, (n_pass, rows), 1)
    slab = lax.broadcasted_iota(jnp.int32, (n_pass, rows), 0)
    alive = (row // WIN == slab) & ((row % WIN) * WINDOW_TOKENS < lens_m)
    live = jnp.where(alive, 1.0, 0.0).astype(F32)
    count = jnp.sum(live, axis=1, keepdims=True)
    p_ref[...] = (jnp.dot(live.astype(BF), coded, preferred_element_type=F32) / count).astype(BF)
    n_q = q_ref.shape[0]
    rowq = lax.broadcasted_iota(jnp.int32, (16, rows), 1)
    slabq = lax.broadcasted_iota(jnp.int32, (16, rows), 0)
    pick = jnp.where(rowq // QLEN == slabq, 1.0, 0.0).astype(BF)
    qs = jnp.dot(pick, coded, preferred_element_type=F32) * (1.0 / QLEN)
    q_ref[:, :width] = qs[:n_q].astype(BF)
    q_ref[:, width:] = lists[...]


def pieces(v):
    a = v.astype(BF)
    rest = v - a.astype(F32)
    b = rest.astype(BF)
    return a, b, (rest - b.astype(F32)).astype(BF)


def score_kernel(place, q_ref, p0, p1, p2, p3, out):
    zh, y, c, m = place[0], place[1], place[2], place[3]
    size, width = p0.shape
    n_q = q_ref.shape[0]
    each = size // N_C
    q = q_ref[:, :width]
    lists = q_ref[:, width:].astype(F32)
    neg = lists[:, :N_NEG] * DIGIT + lists[:, N_NEG : 2 * N_NEG]
    count = lists[:, 2 * N_NEG : 2 * N_NEG + 1]
    pos = lists[:, 2 * N_NEG + 1 : 2 * N_NEG + 2] * DIGIT + lists[:, 2 * N_NEG + 2 : 2 * N_NEG + 3]
    slot = lax.broadcasted_iota(jnp.int32, neg.shape, 1).astype(F32)
    neg = jnp.where(slot < count, neg, -1.0)
    qf = q.astype(F32)
    a = jnp.sqrt(jnp.sum(qf * qf, axis=1, keepdims=True) / width + EPS_UNIT)
    p = jnp.concatenate([p0[...], p1[...], p2[...], p3[...]], axis=0)
    n_p = p.shape[0]
    pf = p.astype(F32)
    sq = pf * pf
    hi = sq.astype(BF)
    lo = (sq - hi.astype(F32)).astype(BF)
    ones = jnp.ones((16, width), BF)
    b2 = lax.dot_general(ones, hi, NT, preferred_element_type=F32)
    b2 = b2 + lax.dot_general(ones, lo, NT, preferred_element_type=F32)
    b = jnp.sqrt(b2[:1] / width + EPS_UNIT)
    dots = lax.dot_general(q, p, NT, preferred_element_type=F32)
    s = dots / (width * SHARPNESS * a * b)
    lane = lax.broadcasted_iota(jnp.int32, (1, n_p), 1)
    line = lax.rem(zh - lane // size + N_ZH, N_ZH)
    core = lax.rem(c + lax.rem(lane, size) // each, N_C)
    number = ((line * N_Y + y) * N_C + core) * (each * N_MP) + m * each + lax.rem(lane, each)
    number = number.astype(F32)
    match = jnp.where(pos == number, 1.0, 0.0).astype(F32)
    cand = jnp.zeros((n_q, n_p), F32)
    for j in range(N_NEG):
        cand = cand + jnp.where(neg[:, j : j + 1] == number, 1.0, 0.0)
    w = jnp.exp(s) * cand
    total = jnp.sum(w, axis=1, keepdims=True)
    score_pos = jnp.sum(s * match, axis=1, keepdims=True)
    unit = 1.0 / (np.float32(width**0.5) * b)
    coef = jnp.concatenate(pieces(w * unit) + pieces(match * unit), axis=0)
    grads = jnp.dot(coef, p, preferred_element_type=F32)
    pull = grads[:n_q] + grads[n_q : 2 * n_q] + grads[2 * n_q : 3 * n_q]
    toward = grads[3 * n_q : 4 * n_q] + grads[4 * n_q : 5 * n_q] + grads[5 * n_q :]
    part = width // N_MP
    own = n_q // N_Y
    wide = lax.broadcasted_iota(jnp.int32, (n_q, 128), 1)
    stats = jnp.where(wide < 64, total, score_pos)
    for g in range(N_GRP):
        for yy in range(N_Y):
            rows = slice(yy * own, (yy + 1) * own)
            for mm in range(N_MP):
                cols = slice(mm * part, (mm + 1) * part)
                d = (g * N_Y + yy) * N_MP + mm
                out[d, 0:own, 0:part] = pull[rows, cols]
                out[d, own : 2 * own, 0:part] = toward[rows, cols]
                out[d, 0:own, part:] = stats[rows]
                out[d, own : 2 * own, part:] = stats[rows]


def final_kernel(arrived, grad, loss):
    peers = arrived.shape[0] // N_GRP
    own, part = grad.shape
    acc = arrived[peers]
    for d in range(peers + 1, 2 * peers):
        acc = acc + arrived[d]
    others = acc[:own, part : part + 1]
    score = acc[:own, part + 64 : part + 65]
    total = others + jnp.exp(score)
    pull, toward = acc[:own, :part], acc[own:, :part]
    grad[...] = (pull / total - toward * (others / total)) / SHARPNESS
    column = jnp.log(total) - score
    diagonal = lax.broadcasted_iota(jnp.int32, (own, 128), 0) == lax.broadcasted_iota(
        jnp.int32, (own, 128), 1
    )
    row = jnp.sum(jnp.where(diagonal, column, 0.0), axis=0, keepdims=True)
    loss[...] = row[:, :own]


def body(states, w_in, b_in, w_out, b_out, ln_gain, ln_bias, lengths, neg_ids, neg_count, pos_ids):
    x = states[0]
    rows, width = x.shape
    hid = b_in.shape[0]
    half = hid // 2
    shard = w_in.shape[0]
    m = lax.axis_index("mp")
    place = jnp.stack([lax.axis_index(a) for a in ("zh", "y", "c", "mp")]).astype(jnp.int32)
    part_rows = rows // N_MP
    part = width // N_MP
    n_pass = part_rows // WIN
    n_own_q = part_rows // QLEN
    own_q = n_own_q * N_MP

    pos = pos_ids[:, None]
    lists = jnp.concatenate(
        [neg_ids // DIGIT, neg_ids % DIGIT, neg_count[:, None], pos // DIGIT, pos % DIGIT], axis=1
    ).astype(BF)
    lists = jnp.pad(lists, ((0, 0), (0, 128 - lists.shape[1])))
    lists = lax.dynamic_slice_in_dim(lists, m * n_own_q, n_own_q, 0)

    w_out_t = w_out.T
    first = jnp.concatenate([w_in, w_out_t[:, :half]], axis=1)
    second = w_out_t[:, half:]
    line = jnp.stack([second] + [shift(second, "y", k) for k in (1, 2, 3)])
    firsts = spread(first, ("grp", "zh"), N_Z)
    firsts = [firsts] + [shift(firsts, "y", k) for k in (1, 2, 3)]
    firsts = firsts + [shift(v, "c", 1) for v in firsts]
    seconds = spread(line, ("grp", "zh"), N_Z)
    seconds = [seconds, shift(seconds, "c", 1)]
    weights = pltpu.VMEM((N_Z, N_Y * N_C, shard, hid), BF)
    own, s1, s2, s3 = pl.pallas_call(
        ffn_kernel,
        out_shape=[jax.ShapeDtypeStruct((part_rows, width), F32)]
        + [jax.ShapeDtypeStruct((part_rows, width), BF)] * 3,
        in_specs=[SMEM, VMEM, VMEM] + [ANY] * 10,
        out_specs=[VMEM] * 4,
        scratch_shapes=[
            weights,
            weights,
            pltpu.VMEM((rows, hid), BF),
            pltpu.VMEM((rows, width), F32),
            pltpu.SemaphoreType.DMA((24,)),
        ],
        compiler_params=params(),
        cost_estimate=cost(4 * rows * width * hid, 8 << 20),
        name="ffn",
    )(place, x, b_in[None], *firsts, *seconds)
    r2, r1, r3 = shift(s2, "mp", 2), shift(s1, "mp", 1), shift(s3, "mp", 3)

    *enc, passages, queries = pl.pallas_call(
        norm_kernel,
        out_shape=[jax.ShapeDtypeStruct((part_rows, part), BF)] * 4
        + [
            jax.ShapeDtypeStruct((n_pass, width), BF),
            jax.ShapeDtypeStruct((n_own_q, width + 128), BF),
        ],
        in_specs=[SMEM] + [VMEM] * 10,
        out_specs=[VMEM] * 6,
        scratch_shapes=[pltpu.VMEM((part_rows, width), BF)],
        compiler_params=params(),
        cost_estimate=cost(2 * part_rows * width * 64, 3 << 20),
        name="norm",
    )(place, own, r1, r2, r3, x, b_out[None], ln_gain[None], ln_bias[None], lengths[:, None], lists)

    peers = N_GRP * N_Y * N_MP
    arrived_q = spread(queries, ("grp", "y", "mp"), peers)
    q_all = arrived_q[: peers // N_GRP].reshape(own_q * N_Y, width + 128)
    pair = jnp.concatenate([passages, shift(passages, "c", 1)], axis=0)
    lines = [pair] + [shift_refresh(pair, "zh", k) for k in (1, 2, 3)]
    shares = pl.pallas_call(
        score_kernel,
        out_shape=jax.ShapeDtypeStruct((peers, 2 * own_q, part + 128), F32),
        in_specs=[SMEM] + [VMEM] * 5,
        out_specs=VMEM,
        compiler_params=params(),
        cost_estimate=cost(2 * 256 * width * 300, 3 << 20),
        name="score",
    )(place, q_all, *lines)
    enc, shares = lax.optimization_barrier((enc, shares))
    arrived = lax.all_to_all(shares, ("grp", "y", "mp"), 0, 0, tiled=True)
    grad, loss = pl.pallas_call(
        final_kernel,
        out_shape=[
            jax.ShapeDtypeStruct((own_q, part), F32),
            jax.ShapeDtypeStruct((1, own_q), F32),
        ],
        in_specs=[VMEM],
        out_specs=[VMEM] * 2,
        compiler_params=params(),
        name="final",
    )(arrived)

    placed = [enc[0]] + [shift(enc[k], "mp", k) for k in (1, 2, 3)]
    encoded = jnp.zeros((N_MP, part_rows, part), BF)
    for k in range(N_MP):
        encoded = lax.dynamic_update_slice_in_dim(encoded, placed[k][None], (m - k) % N_MP, 0)
    return encoded.reshape(1, rows, part), grad, loss.reshape(own_q)


def solution(mesh):
    fine = Mesh(
        mesh.devices.reshape(N_GRP, N_ZH, N_Y, N_C, N_MP), ("grp", "zh", "y", "c", "mp")
    )
    dp = ("zh", "y", "c")
    placed = (
        P("grp", dp, None),
        P(("grp",) + dp, "mp"),
        P("mp"),
        P("mp", ("grp",) + dp),
        P(),
        P(),
        P(),
        P(dp),
        P(dp, None),
        P(dp),
        P(dp),
    )
    return jax.shard_map(
        body,
        mesh=fine,
        in_specs=placed,
        out_specs=(P("grp", dp, "mp"), P(dp, "mp"), P(dp)),
        check_vma=False,
    )
```

```python
import jax
import jax.numpy as jnp
import numpy as np
from jax import lax
from jax.experimental import pallas as pl
from jax.experimental.pallas import tpu as pltpu
from jax.sharding import Mesh, PartitionSpec as P

WIN = 4
QLEN = 64
WINDOW_TOKENS = 128
SHARPNESS = 0.05
EPS_NORM = 1e-05
EPS_UNIT = 1e-06

N_GRP, N_ZH, N_Y, N_C, N_MP = 2, 4, 4, 2, 4
N_Z = N_GRP * N_ZH
BF = jnp.bfloat16
F32 = jnp.float32
VMEM = pl.BlockSpec(memory_space=pltpu.VMEM)
SMEM = pl.BlockSpec(memory_space=pltpu.SMEM)
ANY = pl.BlockSpec(memory_space=pl.ANY)
HBM = pl.BlockSpec(memory_space=pltpu.HBM)
NT = (((1,), (1,)), ((), ()))
N_NEG = 32
DIGIT = 64


def params():
    return pltpu.CompilerParams(vmem_limit_bytes=40 * 1024 * 1024)


def cost(flops, size):
    return pl.CostEstimate(flops=flops, bytes_accessed=size, transcendentals=0)


def shift(block, axis, distance):
    n = lax.axis_size(axis)
    return lax.ppermute(block, axis, [(i, (i + distance) % n) for i in range(n)])


def at(axis):
    return lax.axis_index(axis)


def iota(shape, axis):
    return lax.broadcasted_iota(jnp.int32, shape, axis)


def onehot(hit):
    return jnp.where(hit, 1.0, 0.0).astype(BF)


def pack_kernel(w_in, w_out_t, packed, sems):
    shard = w_in.shape[0]
    copies = []
    for z in range(packed.shape[0]):
        copies.append(pltpu.make_async_copy(w_in, packed.at[z, 0:shard], sems.at[2 * z]))
        copies.append(
            pltpu.make_async_copy(w_out_t, packed.at[z, shard : 2 * shard], sems.at[2 * z + 1])
        )
    for copy in copies:
        copy.start()
    for copy in copies:
        copy.wait()


def slots():
    y, c = at("y"), at("c")
    found = []
    for other in range(N_C):
        core = c if other == 0 else 1 - c
        for k in range(N_Y):
            found.append(lax.rem(y - k + N_Y, N_Y) * N_C + core)
    return found


def ffn_kernel(x_any, b_any, *rest):
    sources, small = rest[:8], rest[8:15]
    own_ref, s1, s2, s3 = rest[15:19]
    small_out = rest[19:26]
    w1, w2, x_ref, b_ref, hidden, total, sems = rest[26:]
    m = at("mp")
    hid = hidden.shape[1]
    shard = w1.shape[2]
    early = [
        pltpu.make_async_copy(x_any, x_ref, sems.at[16]),
        pltpu.make_async_copy(b_any, b_ref, sems.at[17]),
    ]
    late = []
    for i, slot in enumerate(slots()):
        early.append(
            pltpu.make_async_copy(sources[i].at[:, 0:shard], w1.at[:, slot], sems.at[2 * i])
        )
        late.append(
            pltpu.make_async_copy(
                sources[i].at[:, shard : 2 * shard], w2.at[:, slot], sems.at[2 * i + 1]
            )
        )
    for i, (source, target) in enumerate(zip(small, small_out)):
        late.append(pltpu.make_async_copy(source, target, sems.at[18 + i]))
    for copy in early + late:
        copy.start()
    for copy in early:
        copy.wait()
    depth = x_ref.shape[1]
    tile = 256
    for t in range(hid // tile):
        cols = slice(t * tile, (t + 1) * tile)
        w = w1[:, :, :, cols].reshape(depth, tile)
        pre = jnp.dot(x_ref[...], w, preferred_element_type=F32) + b_ref[:, cols]
        hidden[:, cols] = (0.5 * pre * (1.0 + lax.erf(pre * np.float32(0.5**0.5)))).astype(BF)
    for copy in late:
        copy.wait()
    planes = tile // (w2.shape[1] * w2.shape[2])
    for t in range(total.shape[1] // tile):
        w = w2[t * planes : (t + 1) * planes].reshape(tile, hid)
        total[:, t * tile : (t + 1) * tile] = lax.dot_general(
            hidden[...], w, NT, preferred_element_type=F32
        )
    rows = own_ref.shape[0]
    for k, out in ((2, s2), (1, s1), (3, s3), (0, own_ref)):
        j = lax.rem(m + k, N_MP)
        block = pl.ds(pl.multiple_of(j * rows, rows), rows)
        if k == 0:
            out[...] = total[block, :] + x_ref[block, :].astype(F32)
        else:
            out[...] = total[block, :].astype(BF)


def pieces(v):
    a = v.astype(BF)
    rest = v - a.astype(F32)
    b = rest.astype(BF)
    return a, b, (rest - b.astype(F32)).astype(BF)


def norm_kernel(
    own, r1, r2, r3, b_out, gain, bias, lens, negs, counts, poss, p_ref, send
):
    m = at("mp")
    rows, width = own.shape
    summed = own[...] + r1[...].astype(F32) + r2[...].astype(F32) + r3[...].astype(F32)
    summed = summed + b_out[...]
    center = jnp.mean(summed, axis=1, keepdims=True)
    off = summed - center
    spread_ = jnp.mean(off * off, axis=1, keepdims=True)
    coded = (off * lax.rsqrt(spread_ + EPS_NORM) * gain[...] + bias[...]).astype(BF)

    n_pass = p_ref.shape[0]
    n_all = lens.shape[1]
    chosen = iota((n_pass, n_all), 1) == iota((n_pass, n_all), 0) + m * n_pass
    length = jnp.sum(jnp.where(chosen, lens[...].astype(F32), 0.0), axis=1, keepdims=True)
    row = iota((n_pass, rows), 1)
    slab = iota((n_pass, rows), 0)
    begin = ((row % WIN) * WINDOW_TOKENS).astype(F32)
    live = jnp.where((row // WIN == slab) & (begin < length), 1.0, 0.0).astype(F32)
    count = jnp.sum(live, axis=1, keepdims=True)
    p = (jnp.dot(live.astype(BF), coded, preferred_element_type=F32) / count).astype(BF)
    p_ref[:, :width] = p
    pf = p.astype(F32)
    square = pieces(jnp.sum(pf * pf, axis=1, keepdims=True))
    lane = iota((n_pass, 128), 1)
    tail = jnp.zeros((n_pass, 128), F32)
    for i, piece in enumerate(square):
        tail = jnp.where(lane == i, piece.astype(F32), tail)
    p_ref[:, width:] = tail.astype(BF)

    pick = onehot(iota((16, rows), 1) // QLEN == iota((16, rows), 0))
    q = (jnp.dot(pick, coded, preferred_element_type=F32) * (1.0 / QLEN)).astype(BF)
    part = send.shape[2]
    block = jnp.zeros((16, part), F32)
    r16, c16 = iota((16, 16), 0), iota((16, 16), 1)
    n_q = rows // QLEN
    for j in range(N_MP):
        move = onehot((r16 == c16 + j * n_q) & (c16 < n_q))
        block = block + jnp.dot(
            move, q[:, j * part : (j + 1) * part], preferred_element_type=F32
        )
    own_q, n_neg = negs.shape
    ids = negs[...]
    diag = iota((own_q, own_q), 0) == iota((own_q, own_q), 1)
    n_used = jnp.sum(jnp.where(diag, counts[...].astype(F32), 0.0), axis=1, keepdims=True)
    pos = jnp.sum(jnp.where(diag, poss[...].astype(F32), 0.0), axis=1, keepdims=True)
    pos = pos.astype(jnp.int32)
    wide = iota((n_neg, part), 1)
    deep = iota((n_neg, part), 0)
    high = (ids // DIGIT).astype(F32).astype(BF)
    low = (ids % DIGIT).astype(F32).astype(BF)
    lists = jnp.dot(high, onehot(wide == deep), preferred_element_type=F32)
    lists = lists + jnp.dot(low, onehot(wide == deep + n_neg), preferred_element_type=F32)
    lane = iota((own_q, part), 1)
    lists = jnp.where(lane == 2 * n_neg, n_used, lists)
    lists = jnp.where(lane == 2 * n_neg + 1, (pos // DIGIT).astype(F32), lists)
    lists = jnp.where(lane == 2 * n_neg + 2, (pos % DIGIT).astype(F32), lists)
    r8, c8 = iota((16, own_q), 0), iota((16, own_q), 1)
    base = N_MP * n_q
    move = onehot((r8 >= base) & (r8 < base + n_q) & (c8 == m * n_q + r8 - base))
    block = (block + jnp.dot(move, lists.astype(BF), preferred_element_type=F32)).astype(BF)
    for g in range(N_GRP):
        for j in range(N_MP):
            send[g * N_MP + j, :rows, :] = coded[:, j * part : (j + 1) * part]
            send[g * N_MP + j, rows:, :] = block


def unpack_kernel(arrived, encoded, q_ref, lists):
    grp = at("grp")
    part = encoded.shape[1]
    rows = encoded.shape[0] // N_MP
    for j in range(N_MP):
        encoded[j * rows : (j + 1) * rows, :] = arrived[grp * N_MP + j, 0:rows, :]
    blocks = arrived[0:N_MP, rows : rows + 16, :].reshape(N_MP * 16, part)
    n_q = rows // QLEN
    shape = (16, N_MP * 16)
    r, c = iota(shape, 0), iota(shape, 1)
    for j in range(N_MP + 1):
        take = onehot((c // 16 == r // n_q) & (c % 16 == j * n_q + r % n_q))
        got = jnp.dot(take, blocks, preferred_element_type=F32)
        if j < N_MP:
            q_ref[:, j * part : (j + 1) * part] = got.astype(BF)
        else:
            lists[...] = got


def score_kernel(q_ref, lists_ref, *rest):
    blocks, out = rest[:-1], rest[-1]
    zh, y, c, m = at("zh"), at("y"), at("c"), at("mp")
    size = blocks[0].shape[0]
    width = q_ref.shape[1]
    each = size // N_ZH
    n_q = out.shape[1] // 2
    q = q_ref[...]
    qf = q.astype(F32)
    a = jnp.sqrt(jnp.sum(qf * qf, axis=1, keepdims=True) / width + EPS_UNIT)[:n_q]
    lists = lists_ref[:n_q, :]
    neg = lists[:, :N_NEG] * DIGIT + lists[:, N_NEG : 2 * N_NEG]
    count = lists[:, 2 * N_NEG : 2 * N_NEG + 1]
    pos = lists[:, 2 * N_NEG + 1 : 2 * N_NEG + 2] * DIGIT + lists[:, 2 * N_NEG + 2 : 2 * N_NEG + 3]
    slot = iota(neg.shape, 1).astype(F32)
    neg = jnp.where(slot < count, neg, -1.0)
    dots, squares = [], []
    first_three = onehot(iota((16, 128), 1) < 3)
    for block in blocks:
        dots.append(
            lax.dot_general(q, block[:, :width], NT, preferred_element_type=F32)[:n_q]
        )
        squares.append(
            lax.dot_general(first_three, block[:, width:], NT, preferred_element_type=F32)[:1]
        )
    dots = jnp.concatenate(dots, axis=1)
    b = jnp.sqrt(jnp.concatenate(squares, axis=1) / width + EPS_UNIT)
    n_p = dots.shape[1]
    s = dots / (width * SHARPNESS * a * b)
    lane = iota((1, n_p), 1)
    per_core = size * N_Y
    core = lax.rem(c + lane // per_core, N_C)
    line = lax.rem(y - lax.rem(lane, per_core) // size + N_Y, N_Y)
    slab = lax.rem(zh - lax.rem(lane, size) // each + N_ZH, N_ZH)
    number = ((slab * N_Y + line) * N_C + core) * (each * N_MP) + m * each + lax.rem(lane, each)
    number = number.astype(F32)
    match = jnp.where(pos == number, 1.0, 0.0).astype(F32)
    cand = jnp.zeros((n_q, n_p), F32)
    for j in range(N_NEG):
        cand = cand + jnp.where(neg[:, j : j + 1] == number, 1.0, 0.0)
    w = jnp.exp(s) * cand
    total = jnp.sum(w, axis=1, keepdims=True)
    score_pos = jnp.sum(s * match, axis=1, keepdims=True)
    unit = 1.0 / (np.float32(width**0.5) * b)
    coef = jnp.concatenate(pieces(w * unit) + pieces(match * unit), axis=0)
    grads = jnp.zeros((6 * n_q, width), F32)
    for i, block in enumerate(blocks):
        grads = grads + jnp.dot(
            coef[:, i * size : (i + 1) * size], block[:, :width], preferred_element_type=F32
        )
    pull = grads[:n_q] + grads[n_q : 2 * n_q] + grads[2 * n_q : 3 * n_q]
    toward = grads[3 * n_q : 4 * n_q] + grads[4 * n_q : 5 * n_q] + grads[5 * n_q :]
    part = width // N_MP
    stats = jnp.where(iota((n_q, 128), 1) < 64, total, score_pos)
    for g in range(N_GRP):
        for mm in range(N_MP):
            cols = slice(mm * part, (mm + 1) * part)
            d = g * N_MP + mm
            out[d, 0:n_q, 0:part] = pull[:, cols]
            out[d, n_q:, 0:part] = toward[:, cols]
            out[d, 0:n_q, part:] = stats
            out[d, n_q:, part:] = stats


def final_kernel(arrived, grad, loss):
    peers = arrived.shape[0] // N_GRP
    own, part = grad.shape
    acc = arrived[peers]
    for d in range(peers + 1, 2 * peers):
        acc = acc + arrived[d]
    others = acc[:own, part : part + 1]
    score = acc[:own, part + 64 : part + 65]
    total = others + jnp.exp(score)
    pull, toward = acc[:own, :part], acc[own:, :part]
    grad[...] = (pull / total - toward * (others / total)) / SHARPNESS
    column = jnp.log(total) - score
    diagonal = iota((own, 128), 0) == iota((own, 128), 1)
    row = jnp.sum(jnp.where(diagonal, column, 0.0), axis=0, keepdims=True)
    loss[...] = row[:, :own]


def body(states, w_in, b_in, w_out, b_out, ln_gain, ln_bias, lengths, neg_ids, neg_count, pos_ids):
    x = states[0]
    rows, width = x.shape
    hid = b_in.shape[0]
    shard = w_in.shape[0]
    part_rows = rows // N_MP
    part = width // N_MP
    n_pass = part_rows // WIN
    own_q = part_rows // QLEN * N_MP
    peers = N_GRP * N_MP
    shape = jax.ShapeDtypeStruct

    packed = pl.pallas_call(
        pack_kernel,
        out_shape=shape((N_Z, 2 * shard, hid), BF),
        in_specs=[HBM] * 2,
        out_specs=VMEM,
        scratch_shapes=[pltpu.SemaphoreType.DMA((2 * N_Z,))],
        compiler_params=params(),
        name="pack",
    )(w_in, w_out.T)
    lines = [lax.all_to_all(packed, ("grp", "zh"), 0, 0, tiled=True)]
    lines = lines + [shift(lines[0], "y", k) for k in (1, 2, 3)]
    lines = lines + [shift(v, "c", 1) for v in lines]
    small = [
        b_out[None],
        ln_gain[None],
        ln_bias[None],
        lengths[None],
        neg_ids,
        neg_count[None],
        pos_ids[None],
    ]
    weights = pltpu.VMEM((N_Z, N_Y * N_C, shard, hid), BF)
    own, s1, s2, s3, *small = pl.pallas_call(
        ffn_kernel,
        out_shape=[shape((part_rows, width), F32)]
        + [shape((part_rows, width), BF)] * 3
        + [shape(v.shape, v.dtype) for v in small],
        in_specs=[HBM] * 2 + [ANY] * 8 + [HBM] * 7,
        out_specs=[VMEM] * 11,
        scratch_shapes=[
            weights,
            weights,
            pltpu.VMEM((rows, width), BF),
            pltpu.VMEM((1, hid), F32),
            pltpu.VMEM((rows, hid), BF),
            pltpu.VMEM((rows, width), F32),
            pltpu.SemaphoreType.DMA((25,)),
        ],
        compiler_params=params(),
        cost_estimate=cost(4 * rows * width * hid, 8 << 20),
        name="ffn",
    )(x, b_in[None], *lines, *small)
    r2, r1, r3 = shift(s2, "mp", 2), shift(s1, "mp", 1), shift(s3, "mp", 3)

    passages, send = pl.pallas_call(
        norm_kernel,
        out_shape=[
            shape((n_pass, width + 128), BF),
            shape((peers, part_rows + 16, part), BF),
        ],
        in_specs=[VMEM] * 11,
        out_specs=[VMEM] * 2,
        compiler_params=params(),
        cost_estimate=cost(2 * part_rows * width * 64, 3 << 20),
        name="norm",
    )(own, r1, r2, r3, *small)

    slab = jnp.concatenate(
        [passages] + [shift(passages, "zh", k) for k in (1, 2, 3)], axis=0
    )
    lines = [slab] + [shift(slab, "y", k) for k in (1, 2, 3)]
    lines = lines + [shift(v, "c", 1) for v in lines]
    arrived = lax.all_to_all(send, ("grp", "mp"), 0, 0, tiled=True)
    encoded, q_all, lists = pl.pallas_call(
        unpack_kernel,
        out_shape=[shape((rows, part), BF), shape((16, width), BF), shape((16, part), F32)],
        in_specs=[VMEM],
        out_specs=[VMEM] * 3,
        compiler_params=params(),
        name="unpack",
    )(arrived)
    shares = pl.pallas_call(
        score_kernel,
        out_shape=shape((peers, 2 * own_q, part + 128), F32),
        in_specs=[VMEM] * 10,
        out_specs=VMEM,
        compiler_params=params(),
        cost_estimate=cost(2 * 1024 * width * 100, 3 << 20),
        name="score",
    )(q_all, lists, *lines)
    arrived = lax.all_to_all(shares, ("grp", "mp"), 0, 0, tiled=True)
    grad, loss = pl.pallas_call(
        final_kernel,
        out_shape=[shape((own_q, part), F32), shape((1, own_q), F32)],
        in_specs=[VMEM],
        out_specs=[VMEM] * 2,
        compiler_params=params(),
        name="final",
    )(arrived)
    return encoded[None], grad, loss.reshape(own_q)


def solution(mesh):
    fine = Mesh(
        mesh.devices.reshape(N_GRP, N_ZH, N_Y, N_C, N_MP), ("grp", "zh", "y", "c", "mp")
    )
    dp = ("zh", "y", "c")
    placed = (
        P("grp", dp, None),
        P(("grp",) + dp, "mp"),
        P("mp"),
        P("mp", ("grp",) + dp),
        P(),
        P(),
        P(),
        P(dp),
        P(dp, None),
        P(dp),
        P(dp),
    )
    return jax.shard_map(
        body,
        mesh=fine,
        in_specs=placed,
        out_specs=(P("grp", dp, "mp"), P(dp, "mp"), P(dp)),
        check_vma=False,
    )
```

```python
import jax
import jax.numpy as jnp
import numpy as np
from jax import lax
from jax.experimental import pallas as pl
from jax.experimental.pallas import tpu as pltpu
from jax.sharding import Mesh, PartitionSpec as P

WIN = 4
QLEN = 64
WINDOW_TOKENS = 128
SHARPNESS = 0.05
EPS_NORM = 1e-05
EPS_UNIT = 1e-06

N_GRP, N_ZH, N_Y, N_C, N_MP = 2, 4, 4, 2, 4
N_Z = N_GRP * N_ZH
BF = jnp.bfloat16
F32 = jnp.float32
VMEM = pl.BlockSpec(memory_space=pltpu.VMEM)
SMEM = pl.BlockSpec(memory_space=pltpu.SMEM)
ANY = pl.BlockSpec(memory_space=pl.ANY)
HBM = pl.BlockSpec(memory_space=pltpu.HBM)
NT = (((1,), (1,)), ((), ()))
N_NEG = 32
DIGIT = 64


def params():
    return pltpu.CompilerParams(vmem_limit_bytes=40 * 1024 * 1024)


def cost(flops, size):
    return pl.CostEstimate(flops=flops, bytes_accessed=size, transcendentals=0)


def shift(block, axis, distance):
    n = lax.axis_size(axis)
    return lax.ppermute(block, axis, [(i, (i + distance) % n) for i in range(n)])


def cross(block, up):
    route = []
    for i in range(N_ZH):
        j = i if up else (i - 1) % N_ZH
        route += [(i, N_ZH + j), (N_ZH + j, i)]
    return lax.ppermute(block, ("grp", "zh"), route)


def reroute(block, target):
    route = []
    for g in range(N_GRP):
        for z in range(N_ZH):
            to_g, to_z = target(g, z)
            route.append((g * N_ZH + z, to_g * N_ZH + to_z % N_ZH))
    return lax.ppermute(block, ("grp", "zh"), route)


def at(axis):
    return lax.axis_index(axis)


def iota(shape, axis):
    return lax.broadcasted_iota(jnp.int32, shape, axis)


def onehot(hit):
    return jnp.where(hit, 1.0, 0.0).astype(BF)


def pack_kernel(w_in, w_out_t, packed, sems):
    shard = w_in.shape[0]
    copies = []
    for z in range(packed.shape[0]):
        copies.append(pltpu.make_async_copy(w_in, packed.at[z, 0:shard], sems.at[2 * z]))
        copies.append(
            pltpu.make_async_copy(w_out_t, packed.at[z, shard : 2 * shard], sems.at[2 * z + 1])
        )
    for copy in copies:
        copy.start()
    for copy in copies:
        copy.wait()


def slots():
    g, y, c = at("grp"), at("y"), at("c")
    found = []
    for other in range(N_C):
        core = c if other == 0 else 1 - c
        for far in range(N_GRP):
            group = g if far == 0 else 1 - g
            for k in range(N_Y):
                found.append((group, lax.rem(y - k + N_Y, N_Y) * N_C + core))
    return found


def ffn_kernel(x_any, b_any, *rest):
    sources, small = rest[:16], rest[16:23]
    own_ref, s1, s2, s3 = rest[23:27]
    small_out = rest[27:34]
    w, x_ref, b_ref, hidden, total, sems = rest[34:]
    m = at("mp")
    hid = hidden.shape[1]
    shard = w.shape[3] // 2
    early = [
        pltpu.make_async_copy(x_any, x_ref, sems.at[32]),
        pltpu.make_async_copy(b_any, b_ref, sems.at[33]),
    ]
    late = []
    for i, (group, slot) in enumerate(slots()):
        early.append(
            pltpu.make_async_copy(sources[i], w.at[group, :, slot], sems.at[i])
        )
    for i, (source, target) in enumerate(zip(small, small_out)):
        late.append(pltpu.make_async_copy(source, target, sems.at[34 + i]))
    for copy in early + late:
        copy.start()
    for copy in early:
        copy.wait()
    depth = x_ref.shape[1]
    tile = 256
    for t in range(hid // tile):
        cols = slice(t * tile, (t + 1) * tile)
        w_in = w[:, :, :, 0:shard, cols].reshape(depth, tile)
        pre = jnp.dot(x_ref[...], w_in, preferred_element_type=F32) + b_ref[:, cols]
        hidden[:, cols] = (0.5 * pre * (1.0 + lax.erf(pre * np.float32(0.5**0.5)))).astype(BF)
    for copy in late:
        copy.wait()
    planes = tile // (w.shape[2] * shard)
    per_group = w.shape[1] // planes
    for t in range(total.shape[1] // tile):
        begin = t % per_group * planes
        w_out = w[t // per_group, begin : begin + planes, :, shard:, :].reshape(tile, hid)
        total[:, t * tile : (t + 1) * tile] = lax.dot_general(
            hidden[...], w_out, NT, preferred_element_type=F32
        )
    rows = own_ref.shape[0]
    for k, out in ((2, s2), (1, s1), (3, s3), (0, own_ref)):
        j = lax.rem(m + k, N_MP)
        block = pl.ds(pl.multiple_of(j * rows, rows), rows)
        if k == 0:
            out[...] = total[block, :] + x_ref[block, :].astype(F32)
        else:
            out[...] = total[block, :].astype(BF)


def pieces(v):
    a = v.astype(BF)
    rest = v - a.astype(F32)
    b = rest.astype(BF)
    return a, b, (rest - b.astype(F32)).astype(BF)


def norm_kernel(
    own, r1, r2, r3, b_out, gain, bias, lens, negs, counts, poss, p_ref, send
):
    m = at("mp")
    rows, width = own.shape
    summed = own[...] + r1[...].astype(F32) + r2[...].astype(F32) + r3[...].astype(F32)
    summed = summed + b_out[...]
    center = jnp.mean(summed, axis=1, keepdims=True)
    off = summed - center
    spread_ = jnp.mean(off * off, axis=1, keepdims=True)
    coded = (off * lax.rsqrt(spread_ + EPS_NORM) * gain[...] + bias[...]).astype(BF)

    n_pass = p_ref.shape[0]
    n_all = lens.shape[1]
    chosen = iota((n_pass, n_all), 1) == iota((n_pass, n_all), 0) + m * n_pass
    length = jnp.sum(jnp.where(chosen, lens[...].astype(F32), 0.0), axis=1, keepdims=True)
    row = iota((n_pass, rows), 1)
    slab = iota((n_pass, rows), 0)
    begin = ((row % WIN) * WINDOW_TOKENS).astype(F32)
    live = jnp.where((row // WIN == slab) & (begin < length), 1.0, 0.0).astype(F32)
    count = jnp.sum(live, axis=1, keepdims=True)
    p = (jnp.dot(live.astype(BF), coded, preferred_element_type=F32) / count).astype(BF)
    p_ref[:, :width] = p
    pf = p.astype(F32)
    square = pieces(jnp.sum(pf * pf, axis=1, keepdims=True))
    lane = iota((n_pass, 128), 1)
    tail = jnp.zeros((n_pass, 128), F32)
    for i, piece in enumerate(square):
        tail = jnp.where(lane == i, piece.astype(F32), tail)
    p_ref[:, width:] = tail.astype(BF)

    pick = onehot(iota((16, rows), 1) // QLEN == iota((16, rows), 0))
    q = (jnp.dot(pick, coded, preferred_element_type=F32) * (1.0 / QLEN)).astype(BF)
    part = send.shape[2]
    block = jnp.zeros((16, part), F32)
    r16, c16 = iota((16, 16), 0), iota((16, 16), 1)
    n_q = rows // QLEN
    for j in range(N_MP):
        move = onehot((r16 == c16 + j * n_q) & (c16 < n_q))
        block = block + jnp.dot(
            move, q[:, j * part : (j + 1) * part], preferred_element_type=F32
        )
    own_q, n_neg = negs.shape
    ids = negs[...]
    diag = iota((own_q, own_q), 0) == iota((own_q, own_q), 1)
    n_used = jnp.sum(jnp.where(diag, counts[...].astype(F32), 0.0), axis=1, keepdims=True)
    pos = jnp.sum(jnp.where(diag, poss[...].astype(F32), 0.0), axis=1, keepdims=True)
    pos = pos.astype(jnp.int32)
    wide = iota((n_neg, part), 1)
    deep = iota((n_neg, part), 0)
    high = (ids // DIGIT).astype(F32).astype(BF)
    low = (ids % DIGIT).astype(F32).astype(BF)
    lists = jnp.dot(high, onehot(wide == deep), preferred_element_type=F32)
    lists = lists + jnp.dot(low, onehot(wide == deep + n_neg), preferred_element_type=F32)
    lane = iota((own_q, part), 1)
    lists = jnp.where(lane == 2 * n_neg, n_used, lists)
    lists = jnp.where(lane == 2 * n_neg + 1, (pos // DIGIT).astype(F32), lists)
    lists = jnp.where(lane == 2 * n_neg + 2, (pos % DIGIT).astype(F32), lists)
    r8, c8 = iota((16, own_q), 0), iota((16, own_q), 1)
    base = N_MP * n_q
    move = onehot((r8 >= base) & (r8 < base + n_q) & (c8 == m * n_q + r8 - base))
    block = (block + jnp.dot(move, lists.astype(BF), preferred_element_type=F32)).astype(BF)
    for g in range(N_GRP):
        for j in range(N_MP):
            send[g * N_MP + j, :rows, :] = coded[:, j * part : (j + 1) * part]
            send[g * N_MP + j, rows:, :] = block


def unpack_kernel(arrived, encoded, q_ref, lists):
    grp = at("grp")
    part = encoded.shape[1]
    rows = encoded.shape[0] // N_MP
    for j in range(N_MP):
        encoded[j * rows : (j + 1) * rows, :] = arrived[grp * N_MP + j, 0:rows, :]
    blocks = arrived[0:N_MP, rows : rows + 16, :].reshape(N_MP * 16, part)
    n_q = rows // QLEN
    shape = (16, N_MP * 16)
    r, c = iota(shape, 0), iota(shape, 1)
    for j in range(N_MP + 1):
        take = onehot((c // 16 == r // n_q) & (c % 16 == j * n_q + r % n_q))
        got = jnp.dot(take, blocks, preferred_element_type=F32)
        if j < N_MP:
            q_ref[:, j * part : (j + 1) * part] = got.astype(BF)
        else:
            lists[...] = got


def score_kernel(q_ref, lists_ref, *rest):
    blocks, out = rest[:-1], rest[-1]
    g, zh, y, c, m = at("grp"), at("zh"), at("y"), at("c"), at("mp")
    size = blocks[0].shape[0]
    width = q_ref.shape[1]
    each = size // N_GRP
    n_q = out.shape[1] // 2
    q = q_ref[...]
    qf = q.astype(F32)
    a = jnp.sqrt(jnp.sum(qf * qf, axis=1, keepdims=True) / width + EPS_UNIT)[:n_q]
    lists = lists_ref[:n_q, :]
    neg = lists[:, :N_NEG] * DIGIT + lists[:, N_NEG : 2 * N_NEG]
    count = lists[:, 2 * N_NEG : 2 * N_NEG + 1]
    pos = lists[:, 2 * N_NEG + 1 : 2 * N_NEG + 2] * DIGIT + lists[:, 2 * N_NEG + 2 : 2 * N_NEG + 3]
    slot = iota(neg.shape, 1).astype(F32)
    neg = jnp.where(slot < count, neg, -1.0)
    dots, squares = [], []
    first_three = onehot(iota((16, 128), 1) < 3)
    for block in blocks:
        dots.append(
            lax.dot_general(q, block[:, :width], NT, preferred_element_type=F32)[:n_q]
        )
        squares.append(
            lax.dot_general(first_three, block[:, width:], NT, preferred_element_type=F32)[:1]
        )
    dots = jnp.concatenate(dots, axis=1)
    b = jnp.sqrt(jnp.concatenate(squares, axis=1) / width + EPS_UNIT)
    n_p = dots.shape[1]
    s = dots / (width * SHARPNESS * a * b)
    lane = iota((1, n_p), 1)
    per_core = size * N_Y
    core = lax.rem(c + lane // per_core, N_C)
    line = lax.rem(y - lax.rem(lane, per_core) // size + N_Y, N_Y)
    piece = lax.rem(lane, size) // each
    slab = lax.rem(zh + g * piece + (1 - g) * (N_ZH - 1) * (1 + piece), N_ZH)
    number = ((slab * N_Y + line) * N_C + core) * (each * N_MP) + m * each + lax.rem(lane, each)
    number = number.astype(F32)
    match = jnp.where(pos == number, 1.0, 0.0).astype(F32)
    cand = jnp.zeros((n_q, n_p), F32)
    for j in range(N_NEG):
        cand = cand + jnp.where(neg[:, j : j + 1] == number, 1.0, 0.0)
    w = jnp.exp(s) * cand
    total = jnp.sum(w, axis=1, keepdims=True)
    score_pos = jnp.sum(s * match, axis=1, keepdims=True)
    unit = 1.0 / (np.float32(width**0.5) * b)
    coef = jnp.concatenate(pieces(w * unit) + pieces(match * unit), axis=0)
    grads = jnp.zeros((6 * n_q, width), F32)
    for i, block in enumerate(blocks):
        grads = grads + jnp.dot(
            coef[:, i * size : (i + 1) * size], block[:, :width], preferred_element_type=F32
        )
    pull = grads[:n_q] + grads[n_q : 2 * n_q] + grads[2 * n_q : 3 * n_q]
    toward = grads[3 * n_q : 4 * n_q] + grads[4 * n_q : 5 * n_q] + grads[5 * n_q :]
    part = width // N_MP
    stats = jnp.where(iota((n_q, 128), 1) < 64, total, score_pos)
    for g in range(N_GRP):
        for mm in range(N_MP):
            cols = slice(mm * part, (mm + 1) * part)
            d = g * N_MP + mm
            out[d, 0:n_q, 0:part] = pull[:, cols]
            out[d, n_q:, 0:part] = toward[:, cols]
            out[d, 0:n_q, part:] = stats
            out[d, n_q:, part:] = stats


def final_kernel(arrived, grad, loss):
    own, part = grad.shape
    acc = arrived[0]
    for d in range(1, arrived.shape[0]):
        acc = acc + arrived[d]
    others = acc[:own, part : part + 1]
    score = acc[:own, part + 64 : part + 65]
    total = others + jnp.exp(score)
    pull, toward = acc[:own, :part], acc[own:, :part]
    grad[...] = (pull / total - toward * (others / total)) / SHARPNESS
    column = jnp.log(total) - score
    diagonal = iota((own, 128), 0) == iota((own, 128), 1)
    row = jnp.sum(jnp.where(diagonal, column, 0.0), axis=0, keepdims=True)
    loss[...] = row[:, :own]


def body(states, w_in, b_in, w_out, b_out, ln_gain, ln_bias, lengths, neg_ids, neg_count, pos_ids):
    x = states[0]
    rows, width = x.shape
    hid = b_in.shape[0]
    shard = w_in.shape[0]
    part_rows = rows // N_MP
    part = width // N_MP
    n_pass = part_rows // WIN
    own_q = part_rows // QLEN * N_MP
    peers = N_GRP * N_MP
    shape = jax.ShapeDtypeStruct

    packed = pl.pallas_call(
        pack_kernel,
        out_shape=shape((N_ZH, 2 * shard, hid), BF),
        in_specs=[HBM] * 2,
        out_specs=VMEM,
        scratch_shapes=[pltpu.SemaphoreType.DMA((2 * N_ZH,))],
        compiler_params=params(),
        name="pack",
    )(w_in, w_out.T)
    lines = [lax.all_to_all(packed, "zh", 0, 0, tiled=True)]
    lines = lines + [shift(lines[0], "y", k) for k in (1, 2, 3)]
    lines = lines + [cross(v, k % 2 == 0) for k, v in enumerate(lines)]
    lines = lines + [shift(v, "c", 1) for v in lines]
    small = [
        b_out[None],
        ln_gain[None],
        ln_bias[None],
        lengths[None],
        neg_ids,
        neg_count[None],
        pos_ids[None],
    ]
    weights = pltpu.VMEM((N_GRP, N_ZH, N_Y * N_C, 2 * shard, hid), BF)
    own, s1, s2, s3, *small = pl.pallas_call(
        ffn_kernel,
        out_shape=[shape((part_rows, width), F32)]
        + [shape((part_rows, width), BF)] * 3
        + [shape(v.shape, v.dtype) for v in small],
        in_specs=[HBM] * 2 + [ANY] * 16 + [HBM] * 7,
        out_specs=[VMEM] * 11,
        scratch_shapes=[
            weights,
            pltpu.VMEM((rows, width), BF),
            pltpu.VMEM((1, hid), F32),
            pltpu.VMEM((rows, hid), BF),
            pltpu.VMEM((rows, width), F32),
            pltpu.SemaphoreType.DMA((41,)),
        ],
        compiler_params=params(),
        cost_estimate=cost(4 * rows * width * hid, 8 << 20),
        name="ffn",
    )(x, b_in[None], *lines, *small)
    r2, r1, r3 = shift(s2, "mp", 2), shift(s1, "mp", 1), shift(s3, "mp", 3)

    passages, send = pl.pallas_call(
        norm_kernel,
        out_shape=[
            shape((n_pass, width + 128), BF),
            shape((peers, part_rows + 16, part), BF),
        ],
        in_specs=[VMEM] * 11,
        out_specs=[VMEM] * 2,
        compiler_params=params(),
        cost_estimate=cost(2 * part_rows * width * 64, 3 << 20),
        name="norm",
    )(own, r1, r2, r3, *small)

    far = reroute(passages, lambda g, z: (1 - g, z - 2 if g else z + 2))
    mid = reroute(passages, lambda g, z: (g, z - 1))
    near = reroute(passages, lambda g, z: (1 - g, z + 1 if g else z - 1))
    refresh = at("grp") == 1
    slab = jnp.concatenate(
        [jnp.where(refresh, passages, near), jnp.where(refresh, mid, far)], axis=0
    )
    lines = [slab] + [shift(slab, "y", k) for k in (1, 2, 3)]
    lines = lines + [shift(v, "c", 1) for v in lines]
    arrived = lax.all_to_all(send, ("grp", "mp"), 0, 0, tiled=True)
    encoded, q_all, lists = pl.pallas_call(
        unpack_kernel,
        out_shape=[shape((rows, part), BF), shape((16, width), BF), shape((16, part), F32)],
        in_specs=[VMEM],
        out_specs=[VMEM] * 3,
        compiler_params=params(),
        name="unpack",
    )(arrived)
    shares = pl.pallas_call(
        score_kernel,
        out_shape=shape((peers, 2 * own_q, part + 128), F32),
        in_specs=[VMEM] * 10,
        out_specs=VMEM,
        compiler_params=params(),
        cost_estimate=cost(2 * 512 * width * 100, 3 << 20),
        name="score",
    )(q_all, lists, *lines)
    arrived = lax.all_to_all(shares, ("grp", "mp"), 0, 0, tiled=True)
    grad, loss = pl.pallas_call(
        final_kernel,
        out_shape=[shape((own_q, part), F32), shape((1, own_q), F32)],
        in_specs=[VMEM],
        out_specs=[VMEM] * 2,
        compiler_params=params(),
        name="final",
    )(arrived)
    return encoded[None], grad, loss.reshape(own_q)


def solution(mesh):
    fine = Mesh(
        mesh.devices.reshape(N_GRP, N_ZH, N_Y, N_C, N_MP), ("grp", "zh", "y", "c", "mp")
    )
    dp = ("zh", "y", "c")
    placed = (
        P("grp", dp, None),
        P(("grp",) + dp, "mp"),
        P("mp"),
        P("mp", ("grp",) + dp),
        P(),
        P(),
        P(),
        P(dp),
        P(dp, None),
        P(dp),
        P(dp),
    )
    return jax.shard_map(
        body,
        mesh=fine,
        in_specs=placed,
        out_specs=(P("grp", dp, "mp"), P(dp, "mp"), P(dp)),
        check_vma=False,
    )
```

```python
import jax
import jax.numpy as jnp
import numpy as np
from jax import lax
from jax.experimental import pallas as pl
from jax.experimental.pallas import tpu as pltpu
from jax.sharding import Mesh, PartitionSpec as P

WIN = 4
QLEN = 64
WINDOW_TOKENS = 128
SHARPNESS = 0.05
EPS_NORM = 1e-05
EPS_UNIT = 1e-06

N_GRP, N_ZH, N_Y, N_C, N_MP = 2, 4, 4, 2, 4
N_Z = N_GRP * N_ZH
BF = jnp.bfloat16
F32 = jnp.float32
VMEM = pl.BlockSpec(memory_space=pltpu.VMEM)
SMEM = pl.BlockSpec(memory_space=pltpu.SMEM)
ANY = pl.BlockSpec(memory_space=pl.ANY)
HBM = pl.BlockSpec(memory_space=pltpu.HBM)
NT = (((1,), (1,)), ((), ()))
N_NEG = 32
Y_ORDER = (1, 3, 2)
QUERY_ROWS = 2
DIGIT = 64


def params(mib=40):
    return pltpu.CompilerParams(vmem_limit_bytes=mib * 1024 * 1024)


def cost(flops, size):
    return pl.CostEstimate(flops=flops, bytes_accessed=size, transcendentals=0)


def shift(block, axis, distance):
    n = lax.axis_size(axis)
    return lax.ppermute(block, axis, [(i, (i + distance) % n) for i in range(n)])


def cross(block, up):
    route = []
    for i in range(N_ZH):
        j = i if up else (i - 1) % N_ZH
        route += [(i, N_ZH + j), (N_ZH + j, i)]
    return lax.ppermute(block, ("grp", "zh"), route)


def reroute(block, target):
    route = []
    for g in range(N_GRP):
        for z in range(N_ZH):
            to_g, to_z = target(g, z)
            route.append((g * N_ZH + z, to_g * N_ZH + to_z % N_ZH))
    return lax.ppermute(block, ("grp", "zh"), route)


def at(axis):
    return lax.axis_index(axis)


def iota(shape, axis):
    return lax.broadcasted_iota(jnp.int32, shape, axis)


def onehot(hit):
    return jnp.where(hit, 1.0, 0.0).astype(BF)


def pack_kernel(w_in, w_out_t, packed, sems):
    shard = w_in.shape[0]
    copies = []
    for z in range(packed.shape[0]):
        copies.append(pltpu.make_async_copy(w_in, packed.at[z, 0:shard], sems.at[2 * z]))
        copies.append(
            pltpu.make_async_copy(w_out_t, packed.at[z, shard : 2 * shard], sems.at[2 * z + 1])
        )
    for copy in copies:
        copy.start()
    for copy in copies:
        copy.wait()


def stage_kernel(x, b_in, x_out, b_out, sems):
    copies = [
        pltpu.make_async_copy(x, x_out, sems.at[0]),
        pltpu.make_async_copy(b_in, b_out, sems.at[1]),
    ]
    for copy in copies:
        copy.start()
    for copy in copies:
        copy.wait()


def slots():
    g, y, c = at("grp"), at("y"), at("c")
    found = []
    for other in range(N_C):
        core = c if other == 0 else 1 - c
        for far in range(N_GRP):
            group = g if far == 0 else 1 - g
            for k in (0,) + Y_ORDER:
                found.append((group, lax.rem(y - k + N_Y, N_Y) * N_C + core))
    return found


def ffn_kernel(x_ref, b_ref, *rest):
    sources = rest[:16]
    own_ref, s1, s2, s3 = rest[16:20]
    w, hidden, total, sems = rest[20:]
    m = at("mp")
    hid = hidden.shape[1]
    shard = w.shape[3] // 2
    copies = []
    for i, (group, slot) in enumerate(slots()):
        copies.append(pltpu.make_async_copy(sources[i], w.at[group, :, slot], sems.at[i]))
    for copy in copies:
        copy.start()
    for copy in copies:
        copy.wait()
    depth = x_ref.shape[1]
    tile = 256
    for t in range(hid // tile):
        cols = slice(t * tile, (t + 1) * tile)
        w_in = w[:, :, :, 0:shard, cols].reshape(depth, tile)
        pre = jnp.dot(x_ref[...], w_in, preferred_element_type=F32) + b_ref[:, cols]
        hidden[:, cols] = (0.5 * pre * (1.0 + lax.erf(pre * np.float32(0.5**0.5)))).astype(BF)
    planes = tile // (w.shape[2] * shard)
    per_group = w.shape[1] // planes
    for t in range(total.shape[1] // tile):
        begin = t % per_group * planes
        w_out = w[t // per_group, begin : begin + planes, :, shard:, :].reshape(tile, hid)
        total[:, t * tile : (t + 1) * tile] = lax.dot_general(
            hidden[...], w_out, NT, preferred_element_type=F32
        )
    rows = own_ref.shape[0]
    for k, out in ((2, s2), (1, s1), (3, s3), (0, own_ref)):
        j = lax.rem(m + k, N_MP)
        block = pl.ds(pl.multiple_of(j * rows, rows), rows)
        if k == 0:
            out[...] = total[block, :] + x_ref[block, :].astype(F32)
        else:
            out[...] = total[block, :].astype(BF)


def pieces(v):
    a = v.astype(BF)
    rest = v - a.astype(F32)
    b = rest.astype(BF)
    return a, b, (rest - b.astype(F32)).astype(BF)


def prep_kernel(b_out, gain, bias, lens, negs, counts, poss, vectors, live, count, lists_ref):
    m = at("mp")
    n_pass, rows = live.shape
    part = lists_ref.shape[1]
    vectors[0:1, :] = b_out[...]
    vectors[1:2, :] = gain[...]
    vectors[2:3, :] = bias[...]
    n_all = lens.shape[1]
    chosen = iota((n_pass, n_all), 1) == iota((n_pass, n_all), 0) + m * n_pass
    length = jnp.sum(jnp.where(chosen, lens[...].astype(F32), 0.0), axis=1, keepdims=True)
    row = iota((n_pass, rows), 1)
    slab = iota((n_pass, rows), 0)
    begin = ((row % WIN) * WINDOW_TOKENS).astype(F32)
    alive = jnp.where((row // WIN == slab) & (begin < length), 1.0, 0.0).astype(F32)
    live[...] = alive.astype(BF)
    count[...] = jnp.broadcast_to(jnp.sum(alive, axis=1, keepdims=True), count.shape)
    own_q, n_neg = negs.shape
    n_q = own_q // N_MP
    ids = negs[...]
    diag = iota((own_q, own_q), 0) == iota((own_q, own_q), 1)
    n_used = jnp.sum(jnp.where(diag, counts[...].astype(F32), 0.0), axis=1, keepdims=True)
    pos = jnp.sum(jnp.where(diag, poss[...].astype(F32), 0.0), axis=1, keepdims=True)
    pos = pos.astype(jnp.int32)
    wide = iota((n_neg, part), 1)
    deep = iota((n_neg, part), 0)
    high = (ids // DIGIT).astype(F32).astype(BF)
    low = (ids % DIGIT).astype(F32).astype(BF)
    lists = jnp.dot(high, onehot(wide == deep), preferred_element_type=F32)
    lists = lists + jnp.dot(low, onehot(wide == deep + n_neg), preferred_element_type=F32)
    lane = iota((own_q, part), 1)
    lists = jnp.where(lane == 2 * n_neg, n_used, lists)
    lists = jnp.where(lane == 2 * n_neg + 1, (pos // DIGIT).astype(F32), lists)
    lists = jnp.where(lane == 2 * n_neg + 2, (pos % DIGIT).astype(F32), lists)
    r8, c8 = iota((16, own_q), 0), iota((16, own_q), 1)
    base = N_MP * n_q
    move = onehot((r8 >= base) & (r8 < base + n_q) & (c8 == m * n_q + r8 - base))
    lists_ref[...] = jnp.dot(move, lists.astype(BF), preferred_element_type=F32)


def norm_kernel(own, r1, r2, r3, vectors, live, count, lists, p_ref, send):
    rows, width = own.shape
    summed = own[...] + r1[...].astype(F32) + r2[...].astype(F32) + r3[...].astype(F32)
    summed = summed + vectors[0:1, :]
    center = jnp.mean(summed, axis=1, keepdims=True)
    off = summed - center
    spread_ = jnp.mean(off * off, axis=1, keepdims=True)
    coded = (off * lax.rsqrt(spread_ + EPS_NORM) * vectors[1:2, :] + vectors[2:3, :]).astype(BF)

    n_pass = p_ref.shape[0]
    p = (jnp.dot(live[...], coded, preferred_element_type=F32) / count[:, 0:1]).astype(BF)
    p_ref[:, :width] = p
    pf = p.astype(F32)
    square = pieces(jnp.sum(pf * pf, axis=1, keepdims=True))
    lane = iota((n_pass, 128), 1)
    tail = jnp.zeros((n_pass, 128), F32)
    for i, piece in enumerate(square):
        tail = jnp.where(lane == i, piece.astype(F32), tail)
    p_ref[:, width:] = tail.astype(BF)

    pick = onehot(iota((16, rows), 1) // QLEN == iota((16, rows), 0))
    q = (jnp.dot(pick, coded, preferred_element_type=F32) * (1.0 / QLEN)).astype(BF)
    part = send.shape[2]
    block = lists[...]
    r16, c16 = iota((16, 16), 0), iota((16, 16), 1)
    n_q = rows // QLEN
    for j in range(N_MP):
        move = onehot((r16 == c16 + j * n_q) & (c16 < n_q))
        block = block + jnp.dot(
            move, q[:, j * part : (j + 1) * part], preferred_element_type=F32
        )
    block = block.astype(BF)
    for g in range(N_GRP):
        for j in range(N_MP):
            send[g * N_MP + j, :rows, :] = coded[:, j * part : (j + 1) * part]
            send[g * N_MP + j, rows:, :] = block


def unpack_kernel(arrived, encoded):
    grp = at("grp")
    rows = encoded.shape[0] // N_MP
    for j in range(N_MP):
        encoded[j * rows : (j + 1) * rows, :] = arrived[grp * N_MP + j, 0:rows, :]


def query_kernel(arrived, q_ref, lists):
    part = arrived.shape[2]
    held = arrived[0:N_MP, arrived.shape[1] - 16 :, :].reshape(N_MP * 16, part)
    own = QUERY_ROWS
    shape = ((N_MP + 1) * 16, N_MP * 16)
    r, col = iota(shape, 0), iota(shape, 1)
    chunk, row = r // 16, r % 16
    take = onehot((col // 16 == row // own) & (col % 16 == chunk * own + row % own))
    got = jnp.dot(take, held, preferred_element_type=F32)
    for j in range(N_MP):
        q_ref[:, j * part : (j + 1) * part] = got[16 * j : 16 * (j + 1)].astype(BF)
    lists[...] = got[16 * N_MP :]


def score_kernel(q_ref, lists_ref, *rest):
    blocks, out = rest[:-1], rest[-1]
    g, zh, y, c, m = at("grp"), at("zh"), at("y"), at("c"), at("mp")
    size = blocks[0].shape[0]
    each = size // N_GRP
    width = q_ref.shape[1]
    part = width // N_MP
    n_q = out.shape[1] // 2
    q = q_ref[...]
    qf = q.astype(F32)
    a = jnp.sqrt(jnp.sum(qf * qf, axis=1, keepdims=True) / width + EPS_UNIT)[:n_q]
    lists = lists_ref[:n_q, :]
    neg = lists[:, :N_NEG] * DIGIT + lists[:, N_NEG : 2 * N_NEG]
    count = lists[:, 2 * N_NEG : 2 * N_NEG + 1]
    pos = lists[:, 2 * N_NEG + 1 : 2 * N_NEG + 2] * DIGIT + lists[:, 2 * N_NEG + 2 : 2 * N_NEG + 3]
    slot = iota(neg.shape, 1).astype(F32)
    neg = jnp.where(slot < count, neg, -1.0)
    dots, squares = [], []
    first_three = onehot(iota((16, 128), 1) < 3)
    for block in blocks:
        dots.append(
            lax.dot_general(q, block[:, :width], NT, preferred_element_type=F32)[:n_q]
        )
        squares.append(
            lax.dot_general(first_three, block[:, width:], NT, preferred_element_type=F32)[:1]
        )
    dots = jnp.concatenate(dots, axis=1)
    b = jnp.sqrt(jnp.concatenate(squares, axis=1) / width + EPS_UNIT)
    n_p = dots.shape[1]
    s = dots / (width * SHARPNESS * a * b)
    lane = iota((1, n_p), 1)
    per_core = size * N_Y
    core = lax.rem(c + lane // per_core, N_C)
    line = lax.rem(y - lax.rem(lane, per_core) // size + N_Y, N_Y)
    piece = lax.rem(lane, size) // each
    slab = lax.rem(zh + g * piece + (1 - g) * (N_ZH - 1) * (1 + piece), N_ZH)
    number = ((slab * N_Y + line) * N_C + core) * (each * N_MP) + m * each + lax.rem(lane, each)
    number = number.astype(F32)
    match = jnp.where(pos == number, 1.0, 0.0).astype(F32)
    cand = jnp.zeros((n_q, n_p), F32)
    for j in range(N_NEG):
        cand = cand + jnp.where(neg[:, j : j + 1] == number, 1.0, 0.0)
    w = jnp.exp(s) * cand
    total = jnp.sum(w, axis=1, keepdims=True)
    score_pos = jnp.sum(s * match, axis=1, keepdims=True)
    unit = 1.0 / (np.float32(width**0.5) * b)
    coef = jnp.concatenate(pieces(w * unit) + pieces(match * unit), axis=0)
    grads = jnp.zeros((6 * n_q, width), F32)
    for i, block in enumerate(blocks):
        grads = grads + jnp.dot(
            coef[:, i * size : (i + 1) * size], block[:, :width], preferred_element_type=F32
        )
    pull = grads[:n_q] + grads[n_q : 2 * n_q] + grads[2 * n_q : 3 * n_q]
    toward = grads[3 * n_q : 4 * n_q] + grads[4 * n_q : 5 * n_q] + grads[5 * n_q :]
    stats = jnp.where(iota((n_q, 128), 1) < 64, total, score_pos)
    for g in range(N_GRP):
        for mm in range(N_MP):
            cols = slice(mm * part, (mm + 1) * part)
            d = g * N_MP + mm
            out[d, 0:n_q, 0:part] = pull[:, cols]
            out[d, n_q:, 0:part] = toward[:, cols]
            out[d, 0:n_q, part:] = stats
            out[d, n_q:, part:] = stats


def final_kernel(arrived, grad, loss):
    own, part = grad.shape
    acc = arrived[0]
    for d in range(1, arrived.shape[0]):
        acc = acc + arrived[d]
    others = acc[:own, part : part + 1]
    score = acc[:own, part + 64 : part + 65]
    total = others + jnp.exp(score)
    pull, toward = acc[:own, :part], acc[own:, :part]
    grad[...] = (pull / total - toward * (others / total)) / SHARPNESS
    column = jnp.log(total) - score
    diagonal = iota((own, 128), 0) == iota((own, 128), 1)
    row = jnp.sum(jnp.where(diagonal, column, 0.0), axis=0, keepdims=True)
    loss[...] = row[:, :own]


def body(states, w_in, b_in, w_out, b_out, ln_gain, ln_bias, lengths, neg_ids, neg_count, pos_ids):
    x = states[0]
    rows, width = x.shape
    hid = b_in.shape[0]
    shard = w_in.shape[0]
    part_rows = rows // N_MP
    part = width // N_MP
    n_pass = part_rows // WIN
    own_q = part_rows // QLEN * N_MP
    peers = N_GRP * N_MP
    shape = jax.ShapeDtypeStruct

    packed = pl.pallas_call(
        pack_kernel,
        out_shape=shape((N_ZH, 2 * shard, hid), BF),
        in_specs=[HBM] * 2,
        out_specs=VMEM,
        scratch_shapes=[pltpu.SemaphoreType.DMA((2 * N_ZH,))],
        compiler_params=params(60),
        name="pack",
    )(w_in, w_out.T)
    lines = [lax.all_to_all(packed, "zh", 0, 0, tiled=True)]
    x, b_in = pl.pallas_call(
        stage_kernel,
        out_shape=[shape((rows, width), BF), shape((1, hid), F32)],
        in_specs=[HBM] * 2,
        out_specs=[VMEM] * 2,
        scratch_shapes=[pltpu.SemaphoreType.DMA((2,))],
        compiler_params=params(20),
        name="stage",
    )(x, b_in[None])
    lines[0], x, b_in = lax.optimization_barrier((lines[0], x, b_in))
    far = [cross(lines[0], True)]
    for k in Y_ORDER:
        lines.append(shift(lines[0], "y", k))
    far = far + [cross(lines[i], Y_ORDER[i - 1] == 2) for i in (1, 2, 3)]
    lines = lines + far
    lines = lines + [shift(v, "c", 1) for v in lines]
    weights = pltpu.VMEM((N_GRP, N_ZH, N_Y * N_C, 2 * shard, hid), BF)
    own, s1, s2, s3 = pl.pallas_call(
        ffn_kernel,
        out_shape=[shape((part_rows, width), F32)] + [shape((part_rows, width), BF)] * 3,
        in_specs=[VMEM] * 2 + [ANY] * 16,
        out_specs=[VMEM] * 4,
        scratch_shapes=[
            weights,
            pltpu.VMEM((rows, hid), BF),
            pltpu.VMEM((rows, width), F32),
            pltpu.SemaphoreType.DMA((16,)),
        ],
        compiler_params=params(20),
        cost_estimate=cost(4 * rows * width * hid, 8 << 20),
        name="ffn",
    )(x, b_in, *lines)
    r2, r1, r3 = shift(s2, "mp", 2), shift(s1, "mp", 1), shift(s3, "mp", 3)
    small = [
        b_out[None],
        ln_gain[None],
        ln_bias[None],
        lengths[None],
        neg_ids,
        neg_count[None],
        pos_ids[None],
    ]
    r1, *small = lax.optimization_barrier((r1, *small))
    vectors, live, count, lists = pl.pallas_call(
        prep_kernel,
        out_shape=[
            shape((3, width), F32),
            shape((n_pass, part_rows), BF),
            shape((n_pass, 128), F32),
            shape((16, part), F32),
        ],
        in_specs=[VMEM] * 7,
        out_specs=[VMEM] * 4,
        compiler_params=params(),
        name="prep",
    )(*small)

    passages, send = pl.pallas_call(
        norm_kernel,
        out_shape=[
            shape((n_pass, width + 128), BF),
            shape((peers, part_rows + 16, part), BF),
        ],
        in_specs=[VMEM] * 8,
        out_specs=[VMEM] * 2,
        compiler_params=params(),
        cost_estimate=cost(2 * part_rows * width * 64, 3 << 20),
        name="norm",
    )(own, r1, r2, r3, vectors, live, count, lists)

    far = reroute(passages, lambda g, z: (1 - g, z - 2 if g else z + 2))
    mid = reroute(passages, lambda g, z: (g, z - 1))
    near = reroute(passages, lambda g, z: (1 - g, z + 1 if g else z - 1))
    refresh = at("grp") == 1
    slab = jnp.concatenate(
        [jnp.where(refresh, passages, near), jnp.where(refresh, mid, far)], axis=0
    )
    lines = [slab] + [shift(slab, "y", k) for k in (1, 2, 3)]
    arrived = lax.all_to_all(send, ("grp", "mp"), 0, 0, tiled=True)
    q_all, lists = pl.pallas_call(
        query_kernel,
        out_shape=[shape((16, width), BF), shape((16, part), F32)],
        in_specs=[VMEM],
        out_specs=[VMEM] * 2,
        compiler_params=params(),
        name="query",
    )(arrived)
    encoded = pl.pallas_call(
        unpack_kernel,
        out_shape=shape((rows, part), BF),
        in_specs=[VMEM],
        out_specs=VMEM,
        compiler_params=params(),
        name="unpack",
    )(arrived)
    lines[1], q_all, encoded = lax.optimization_barrier((lines[1], q_all, encoded))
    lines = lines + [shift(v, "c", 1) for v in lines]
    shares = pl.pallas_call(
        score_kernel,
        out_shape=shape((peers, 2 * own_q, part + 128), F32),
        in_specs=[VMEM] * 10,
        out_specs=VMEM,
        compiler_params=params(),
        cost_estimate=cost(2 * 512 * width * 100, 3 << 20),
        name="score",
    )(q_all, lists, *lines)
    arrived = lax.all_to_all(shares, ("grp", "mp"), 0, 0, tiled=True)
    grad, loss = pl.pallas_call(
        final_kernel,
        out_shape=[shape((own_q, part), F32), shape((1, own_q), F32)],
        in_specs=[VMEM],
        out_specs=[VMEM] * 2,
        compiler_params=params(),
        name="final",
    )(arrived)
    return encoded[None], grad, loss.reshape(own_q)


def solution(mesh):
    fine = Mesh(
        mesh.devices.reshape(N_GRP, N_ZH, N_Y, N_C, N_MP), ("grp", "zh", "y", "c", "mp")
    )
    dp = ("zh", "y", "c")
    placed = (
        P("grp", dp, None),
        P(("grp",) + dp, "mp"),
        P("mp"),
        P("mp", ("grp",) + dp),
        P(),
        P(),
        P(),
        P(dp),
        P(dp, None),
        P(dp),
        P(dp),
    )
    return jax.shard_map(
        body,
        mesh=fine,
        in_specs=placed,
        out_specs=(P("grp", dp, "mp"), P(dp, "mp"), P(dp)),
        check_vma=False,
    )
```

```python
import jax
import jax.numpy as jnp
import numpy as np
from jax import lax
from jax.experimental import pallas as pl
from jax.experimental.pallas import tpu as pltpu
from jax.sharding import Mesh, PartitionSpec as P

WIN = 4
QLEN = 64
WINDOW_TOKENS = 128
SHARPNESS = 0.05
EPS_NORM = 1e-05
EPS_UNIT = 1e-06

N_GRP, N_ZH, N_Y, N_C, N_MP = 2, 4, 4, 2, 4
N_Z = N_GRP * N_ZH
BF = jnp.bfloat16
F32 = jnp.float32
VMEM = pl.BlockSpec(memory_space=pltpu.VMEM)
SMEM = pl.BlockSpec(memory_space=pltpu.SMEM)
ANY = pl.BlockSpec(memory_space=pl.ANY)
HBM = pl.BlockSpec(memory_space=pltpu.HBM)
NT = (((1,), (1,)), ((), ()))
N_NEG = 32
Y_ORDER = (1, 3, 2)
QUERY_ROWS = 2
DIGIT = 64


def params(mib=40):
    return pltpu.CompilerParams(vmem_limit_bytes=mib * 1024 * 1024)


def cost(flops, size):
    return pl.CostEstimate(flops=flops, bytes_accessed=size, transcendentals=0)


def shift(block, axis, distance):
    n = lax.axis_size(axis)
    return lax.ppermute(block, axis, [(i, (i + distance) % n) for i in range(n)])


def cross(block, up):
    route = []
    for i in range(N_ZH):
        j = i if up else (i - 1) % N_ZH
        route += [(i, N_ZH + j), (N_ZH + j, i)]
    return lax.ppermute(block, ("grp", "zh"), route)


def reroute(block, target):
    route = []
    for g in range(N_GRP):
        for z in range(N_ZH):
            to_g, to_z = target(g, z)
            route.append((g * N_ZH + z, to_g * N_ZH + to_z % N_ZH))
    return lax.ppermute(block, ("grp", "zh"), route)


def at(axis):
    return lax.axis_index(axis)


def iota(shape, axis):
    return lax.broadcasted_iota(jnp.int32, shape, axis)


def onehot(hit):
    return jnp.where(hit, 1.0, 0.0).astype(BF)


def pack_kernel(w_in, w_out_t, packed, held, sems):
    shard = w_in.shape[0]
    n = packed.shape[0]
    copies = [
        pltpu.make_async_copy(w_in, held.at[0:shard], sems.at[n]),
        pltpu.make_async_copy(w_out_t, held.at[shard : 2 * shard], sems.at[n + 1]),
    ]
    for copy in copies:
        copy.start()
    for copy in copies:
        copy.wait()
    copies = [pltpu.make_async_copy(held, packed.at[z], sems.at[z]) for z in range(n)]
    for copy in copies:
        copy.start()
    for copy in copies:
        copy.wait()


def stage_kernel(x, b_in, x_out, b_out, sems):
    copies = [
        pltpu.make_async_copy(x, x_out, sems.at[0]),
        pltpu.make_async_copy(b_in, b_out, sems.at[1]),
    ]
    for copy in copies:
        copy.start()
    for copy in copies:
        copy.wait()


def slots():
    g, y, c = at("grp"), at("y"), at("c")
    found = []
    for other in range(N_C):
        core = c if other == 0 else 1 - c
        for far in range(N_GRP):
            group = g if far == 0 else 1 - g
            for k in (0,) + Y_ORDER:
                found.append((group, lax.rem(y - k + N_Y, N_Y) * N_C + core))
    return found


def ffn_kernel(x_ref, b_ref, *rest):
    sources = rest[:16]
    own_ref, s1, s2, s3 = rest[16:20]
    w, hidden, total, sems = rest[20:]
    m = at("mp")
    hid = hidden.shape[1]
    shard = w.shape[3] // 2
    copies = []
    for i, (group, slot) in enumerate(slots()):
        copies.append(pltpu.make_async_copy(sources[i], w.at[group, :, slot], sems.at[i]))
    for copy in copies:
        copy.start()
    for copy in copies:
        copy.wait()
    depth = x_ref.shape[1]
    tile = 256
    for t in range(hid // tile):
        cols = slice(t * tile, (t + 1) * tile)
        w_in = w[:, :, :, 0:shard, cols].reshape(depth, tile)
        pre = jnp.dot(x_ref[...], w_in, preferred_element_type=F32) + b_ref[:, cols]
        hidden[:, cols] = (0.5 * pre * (1.0 + lax.erf(pre * np.float32(0.5**0.5)))).astype(BF)
    planes = tile // (w.shape[2] * shard)
    per_group = w.shape[1] // planes
    for t in range(total.shape[1] // tile):
        begin = t % per_group * planes
        w_out = w[t // per_group, begin : begin + planes, :, shard:, :].reshape(tile, hid)
        total[:, t * tile : (t + 1) * tile] = lax.dot_general(
            hidden[...], w_out, NT, preferred_element_type=F32
        )
    rows = own_ref.shape[0]
    for k, out in ((2, s2), (1, s1), (3, s3), (0, own_ref)):
        j = lax.rem(m + k, N_MP)
        block = pl.ds(pl.multiple_of(j * rows, rows), rows)
        if k == 0:
            out[...] = total[block, :] + x_ref[block, :].astype(F32)
        else:
            out[...] = total[block, :].astype(BF)


def pieces(v):
    a = v.astype(BF)
    rest = v - a.astype(F32)
    b = rest.astype(BF)
    return a, b, (rest - b.astype(F32)).astype(BF)


def prep_kernel(b_out, gain, bias, lens, negs, counts, poss, vectors, live, count, lists_ref):
    m = at("mp")
    n_pass, rows = live.shape
    part = lists_ref.shape[1]
    vectors[0:1, :] = b_out[...]
    vectors[1:2, :] = gain[...]
    vectors[2:3, :] = bias[...]
    n_all = lens.shape[1]
    chosen = iota((n_pass, n_all), 1) == iota((n_pass, n_all), 0) + m * n_pass
    length = jnp.sum(jnp.where(chosen, lens[...].astype(F32), 0.0), axis=1, keepdims=True)
    row = iota((n_pass, rows), 1)
    slab = iota((n_pass, rows), 0)
    begin = ((row % WIN) * WINDOW_TOKENS).astype(F32)
    alive = jnp.where((row // WIN == slab) & (begin < length), 1.0, 0.0).astype(F32)
    live[...] = alive.astype(BF)
    count[...] = jnp.broadcast_to(jnp.sum(alive, axis=1, keepdims=True), count.shape)
    own_q, n_neg = negs.shape
    n_q = own_q // N_MP
    ids = negs[...]
    diag = iota((own_q, own_q), 0) == iota((own_q, own_q), 1)
    n_used = jnp.sum(jnp.where(diag, counts[...].astype(F32), 0.0), axis=1, keepdims=True)
    pos = jnp.sum(jnp.where(diag, poss[...].astype(F32), 0.0), axis=1, keepdims=True)
    pos = pos.astype(jnp.int32)
    wide = iota((n_neg, part), 1)
    deep = iota((n_neg, part), 0)
    high = (ids // DIGIT).astype(F32).astype(BF)
    low = (ids % DIGIT).astype(F32).astype(BF)
    lists = jnp.dot(high, onehot(wide == deep), preferred_element_type=F32)
    lists = lists + jnp.dot(low, onehot(wide == deep + n_neg), preferred_element_type=F32)
    lane = iota((own_q, part), 1)
    lists = jnp.where(lane == 2 * n_neg, n_used, lists)
    lists = jnp.where(lane == 2 * n_neg + 1, (pos // DIGIT).astype(F32), lists)
    lists = jnp.where(lane == 2 * n_neg + 2, (pos % DIGIT).astype(F32), lists)
    r8, c8 = iota((n_pass, own_q), 0), iota((n_pass, own_q), 1)
    move = onehot((r8 < n_q) & (c8 == m * n_q + r8))
    lists_ref[...] = jnp.dot(move, lists.astype(BF), preferred_element_type=F32).astype(BF)


def norm_kernel(own, r1, r2, r3, vectors, live, count, lists, p_ref, coded_ref):
    rows, width = own.shape
    summed = own[...] + r1[...].astype(F32) + r2[...].astype(F32) + r3[...].astype(F32)
    summed = summed + vectors[0:1, :]
    center = jnp.mean(summed, axis=1, keepdims=True)
    off = summed - center
    spread_ = jnp.mean(off * off, axis=1, keepdims=True)
    coded = (off * lax.rsqrt(spread_ + EPS_NORM) * vectors[1:2, :] + vectors[2:3, :]).astype(BF)

    n_pass = p_ref.shape[0]
    p = (jnp.dot(live[...], coded, preferred_element_type=F32) / count[:, 0:1]).astype(BF)
    n_pass = p_ref.shape[0]
    pf = p.astype(F32)
    square = pieces(jnp.sum(pf * pf, axis=1, keepdims=True))
    lane = iota((n_pass, 128), 1)
    tail = jnp.zeros((n_pass, 128), F32)
    for i, piece in enumerate(square):
        tail = jnp.where(lane == i, piece.astype(F32), tail)
    n_pass = p_ref.shape[0]
    pick = onehot(iota((n_pass, rows), 1) // QLEN == iota((n_pass, rows), 0))
    q = (jnp.dot(pick, coded, preferred_element_type=F32) * (1.0 / QLEN)).astype(BF)
    refresh = at("grp") == 1
    p_ref[:, :width] = jnp.where(refresh, p, q)
    p_ref[:, width:] = jnp.where(refresh, tail.astype(BF), lists[...])
    coded_ref[...] = coded


def send_kernel(coded, mine, came, send):
    rows, width = coded.shape
    part = width // N_MP
    n_q = rows // QLEN
    rider = jnp.where(at("grp") == 1, came[0:16, :], mine[0:16, :])
    parts = [rider[:, j * part : (j + 1) * part] for j in range(N_MP)]
    lists = jnp.concatenate([rider[:, width:], rider[:, width:]], axis=1)
    stacked = jnp.concatenate(parts + [lists], axis=0)
    shape = (16, 16 * (N_MP + 1))
    to, come = iota(shape, 0), iota(shape, 1)
    move = onehot((to == come // 16 * n_q + come % 16) & (come % 16 < n_q))
    block = jnp.dot(move, stacked, preferred_element_type=F32).astype(BF)
    for j in range(N_MP):
        send[j, :rows, :] = coded[:, j * part : (j + 1) * part]
        send[j, rows:, :] = block


def query_kernel(arrived, q_ref, lists):
    part = arrived.shape[2]
    held = arrived[0:N_MP, arrived.shape[1] - 16 :, :].reshape(N_MP * 16, part)
    own = QUERY_ROWS
    shape = ((N_MP + 1) * 16, N_MP * 16)
    r, col = iota(shape, 0), iota(shape, 1)
    chunk, row = r // 16, r % 16
    take = onehot((col // 16 == row // own) & (col % 16 == chunk * own + row % own))
    got = jnp.dot(take, held, preferred_element_type=F32)
    for j in range(N_MP):
        q_ref[:, j * part : (j + 1) * part] = got[16 * j : 16 * (j + 1)].astype(BF)
    lists[...] = got[16 * N_MP :]


def unpack_kernel(arrived, encoded):
    rows = encoded.shape[0] // N_MP
    for j in range(N_MP):
        encoded[j * rows : (j + 1) * rows, :] = arrived[j, 0:rows, :]


def score_kernel(q_ref, lists_ref, *rest):
    blocks, out = rest[:-1], rest[-1]
    g, zh, y, c, m = at("grp"), at("zh"), at("y"), at("c"), at("mp")
    size = blocks[0].shape[0]
    each = size // N_GRP
    width = q_ref.shape[1]
    part = width // N_MP
    n_q = out.shape[1] // 2
    q = q_ref[...]
    qf = q.astype(F32)
    a = jnp.sqrt(jnp.sum(qf * qf, axis=1, keepdims=True) / width + EPS_UNIT)[:n_q]
    lists = lists_ref[:n_q, :]
    neg = lists[:, :N_NEG] * DIGIT + lists[:, N_NEG : 2 * N_NEG]
    count = lists[:, 2 * N_NEG : 2 * N_NEG + 1]
    pos = lists[:, 2 * N_NEG + 1 : 2 * N_NEG + 2] * DIGIT + lists[:, 2 * N_NEG + 2 : 2 * N_NEG + 3]
    slot = iota(neg.shape, 1).astype(F32)
    neg = jnp.where(slot < count, neg, -1.0)
    dots, squares = [], []
    first_three = onehot(iota((16, 128), 1) < 3)
    for block in blocks:
        dots.append(
            lax.dot_general(q, block[:, :width], NT, preferred_element_type=F32)[:n_q]
        )
        squares.append(
            lax.dot_general(first_three, block[:, width:], NT, preferred_element_type=F32)[:1]
        )
    dots = jnp.concatenate(dots, axis=1)
    b = jnp.sqrt(jnp.concatenate(squares, axis=1) / width + EPS_UNIT)
    n_p = dots.shape[1]
    s = dots / (width * SHARPNESS * a * b)
    lane = iota((1, n_p), 1)
    per_core = size * N_Y
    core = lax.rem(c + lane // per_core, N_C)
    turn = lax.rem(lane, per_core) // size
    turn = jnp.where(turn < 2, turn, 5 - turn)
    line = lax.rem(y - turn + N_Y, N_Y)
    piece = lax.rem(lane, size) // each
    slab = lax.rem(zh + g * piece + (1 - g) * (N_ZH - 1) * (1 + piece), N_ZH)
    number = ((slab * N_Y + line) * N_C + core) * (each * N_MP) + m * each + lax.rem(lane, each)
    number = number.astype(F32)
    match = jnp.where(pos == number, 1.0, 0.0).astype(F32)
    cand = jnp.zeros((n_q, n_p), F32)
    for j in range(N_NEG):
        cand = cand + jnp.where(neg[:, j : j + 1] == number, 1.0, 0.0)
    w = jnp.exp(s) * cand
    total = jnp.sum(w, axis=1, keepdims=True)
    score_pos = jnp.sum(s * match, axis=1, keepdims=True)
    unit = 1.0 / (np.float32(width**0.5) * b)
    coef = jnp.concatenate(pieces(w * unit) + pieces(match * unit), axis=0)
    grads = jnp.zeros((6 * n_q, width), F32)
    for i, block in enumerate(blocks):
        grads = grads + jnp.dot(
            coef[:, i * size : (i + 1) * size], block[:, :width], preferred_element_type=F32
        )
    pull = grads[:n_q] + grads[n_q : 2 * n_q] + grads[2 * n_q : 3 * n_q]
    toward = grads[3 * n_q : 4 * n_q] + grads[4 * n_q : 5 * n_q] + grads[5 * n_q :]
    stats = jnp.where(iota((n_q, 128), 1) < 64, total, score_pos)
    for g in range(N_GRP):
        for mm in range(N_MP):
            cols = slice(mm * part, (mm + 1) * part)
            d = g * N_MP + mm
            out[d, 0:n_q, 0:part] = pull[:, cols]
            out[d, n_q:, 0:part] = toward[:, cols]
            out[d, 0:n_q, part:] = stats
            out[d, n_q:, part:] = stats


def final_kernel(arrived, grad, loss):
    own, part = grad.shape
    acc = arrived[0]
    for d in range(1, arrived.shape[0]):
        acc = acc + arrived[d]
    others = acc[:own, part : part + 1]
    score = acc[:own, part + 64 : part + 65]
    total = others + jnp.exp(score)
    pull, toward = acc[:own, :part], acc[own:, :part]
    grad[...] = (pull / total - toward * (others / total)) / SHARPNESS
    column = jnp.log(total) - score
    diagonal = iota((own, 128), 0) == iota((own, 128), 1)
    row = jnp.sum(jnp.where(diagonal, column, 0.0), axis=0, keepdims=True)
    loss[...] = row[:, :own]


def body(states, w_in, b_in, w_out, b_out, ln_gain, ln_bias, lengths, neg_ids, neg_count, pos_ids):
    x = states[0]
    rows, width = x.shape
    hid = b_in.shape[0]
    shard = w_in.shape[0]
    part_rows = rows // N_MP
    part = width // N_MP
    n_pass = part_rows // WIN
    own_q = part_rows // QLEN * N_MP
    peers = N_GRP * N_MP
    shape = jax.ShapeDtypeStruct

    packed = pl.pallas_call(
        pack_kernel,
        out_shape=shape((N_ZH, 2 * shard, hid), BF),
        in_specs=[HBM] * 2,
        out_specs=VMEM,
        scratch_shapes=[
            pltpu.VMEM((2 * shard, hid), BF),
            pltpu.SemaphoreType.DMA((N_ZH + 2,)),
        ],
        compiler_params=params(60),
        name="pack",
    )(w_in, w_out.T)
    lines = [lax.all_to_all(packed, "zh", 0, 0, tiled=True)]
    x, b_in = pl.pallas_call(
        stage_kernel,
        out_shape=[shape((rows, width), BF), shape((1, hid), F32)],
        in_specs=[HBM] * 2,
        out_specs=[VMEM] * 2,
        scratch_shapes=[pltpu.SemaphoreType.DMA((2,))],
        compiler_params=params(20),
        name="stage",
    )(x, b_in[None])
    lines[0], x, b_in = lax.optimization_barrier((lines[0], x, b_in))
    far = [cross(lines[0], True)]
    for k in Y_ORDER:
        lines.append(shift(lines[0], "y", k))
    far = far + [cross(lines[i], Y_ORDER[i - 1] == 2) for i in (1, 2, 3)]
    lines = lines + far
    lines = lines + [shift(v, "c", 1) for v in lines]
    weights = pltpu.VMEM((N_GRP, N_ZH, N_Y * N_C, 2 * shard, hid), BF)
    own, s1, s2, s3 = pl.pallas_call(
        ffn_kernel,
        out_shape=[shape((part_rows, width), F32)] + [shape((part_rows, width), BF)] * 3,
        in_specs=[VMEM] * 2 + [ANY] * 16,
        out_specs=[VMEM] * 4,
        scratch_shapes=[
            weights,
            pltpu.VMEM((rows, hid), BF),
            pltpu.VMEM((rows, width), F32),
            pltpu.SemaphoreType.DMA((16,)),
        ],
        compiler_params=params(20),
        cost_estimate=cost(4 * rows * width * hid, 8 << 20),
        name="ffn",
    )(x, b_in, *lines)
    r1, r3, r2 = shift(s1, "mp", 1), shift(s3, "mp", 3), shift(s2, "mp", 2)
    small = [
        b_out[None],
        ln_gain[None],
        ln_bias[None],
        lengths[None],
        neg_ids,
        neg_count[None],
        pos_ids[None],
    ]
    r1, *small = lax.optimization_barrier((r1, *small))
    vectors, live, count, lists = pl.pallas_call(
        prep_kernel,
        out_shape=[
            shape((3, width), F32),
            shape((n_pass, part_rows), BF),
            shape((n_pass, 128), F32),
            shape((n_pass, 128), BF),
        ],
        in_specs=[VMEM] * 7,
        out_specs=[VMEM] * 4,
        compiler_params=params(),
        name="prep",
    )(*small)

    passages, coded = pl.pallas_call(
        norm_kernel,
        out_shape=[
            shape((n_pass, width + 128), BF),
            shape((part_rows, width), BF),
        ],
        in_specs=[VMEM] * 8,
        out_specs=[VMEM] * 2,
        compiler_params=params(),
        cost_estimate=cost(2 * part_rows * width * 64, 3 << 20),
        name="norm",
    )(own, r1, r3, r2, vectors, live, count, lists)

    near = reroute(passages, lambda g, z: (1 - g, z + 1 if g else z))
    mid = reroute(passages, lambda g, z: (g, z - 1))
    far = reroute(passages, lambda g, z: (1 - g, z - 2 if g else z + 2))
    refresh = at("grp") == 1
    slab = jnp.concatenate(
        [jnp.where(refresh, passages, near), jnp.where(refresh, mid, far)], axis=0
    )
    lines = [slab] + [shift(slab, "y", k) for k in Y_ORDER]
    send = pl.pallas_call(
        send_kernel,
        out_shape=shape((N_MP, part_rows + 16, part), BF),
        in_specs=[VMEM] * 3,
        out_specs=VMEM,
        compiler_params=params(),
        name="send",
    )(coded, passages, near)
    arrived = lax.all_to_all(send, "mp", 0, 0, tiled=True)
    q_all, lists = pl.pallas_call(
        query_kernel,
        out_shape=[shape((16, width), BF), shape((16, part), F32)],
        in_specs=[VMEM],
        out_specs=[VMEM] * 2,
        compiler_params=params(),
        name="query",
    )(arrived)
    encoded = pl.pallas_call(
        unpack_kernel,
        out_shape=shape((rows, part), BF),
        in_specs=[VMEM],
        out_specs=VMEM,
        compiler_params=params(),
        name="unpack",
    )(arrived)
    lines[3], q_all = lax.optimization_barrier((lines[3], q_all))
    lines[2], encoded = lax.optimization_barrier((lines[2], encoded))
    lines = lines + [shift(v, "c", 1) for v in lines]
    shares = pl.pallas_call(
        score_kernel,
        out_shape=shape((peers, 2 * own_q, part + 128), F32),
        in_specs=[VMEM] * 10,
        out_specs=VMEM,
        compiler_params=params(),
        cost_estimate=cost(2 * 512 * width * 100, 3 << 20),
        name="score",
    )(q_all, lists, *lines)
    arrived = lax.all_to_all(shares, ("grp", "mp"), 0, 0, tiled=True)
    grad, loss = pl.pallas_call(
        final_kernel,
        out_shape=[shape((own_q, part), F32), shape((1, own_q), F32)],
        in_specs=[VMEM],
        out_specs=[VMEM] * 2,
        compiler_params=params(),
        name="final",
    )(arrived)
    return encoded[None], grad, loss.reshape(own_q)


def solution(mesh):
    fine = Mesh(
        mesh.devices.reshape(N_GRP, N_ZH, N_Y, N_C, N_MP), ("grp", "zh", "y", "c", "mp")
    )
    dp = ("zh", "y", "c")
    placed = (
        P("grp", dp, None),
        P(("grp",) + dp, "mp"),
        P("mp"),
        P("mp", ("grp",) + dp),
        P(),
        P(),
        P(),
        P(dp),
        P(dp, None),
        P(dp),
        P(dp),
    )
    return jax.shard_map(
        body,
        mesh=fine,
        in_specs=placed,
        out_specs=(P("grp", dp, "mp"), P(dp, "mp"), P(dp)),
        check_vma=False,
    )
```

```python
import jax
import jax.numpy as jnp
import numpy as np
from jax import lax
from jax.experimental import pallas as pl
from jax.experimental.pallas import tpu as pltpu
from jax.sharding import Mesh, PartitionSpec as P

WIN = 4
QLEN = 64
WINDOW_TOKENS = 128
SHARPNESS = 0.05
EPS_NORM = 1e-05
EPS_UNIT = 1e-06

N_GRP, N_ZH, N_Y, N_C, N_MP = 2, 4, 4, 2, 4
N_Z = N_GRP * N_ZH
BF = jnp.bfloat16
F32 = jnp.float32
VMEM = pl.BlockSpec(memory_space=pltpu.VMEM)
SMEM = pl.BlockSpec(memory_space=pltpu.SMEM)
ANY = pl.BlockSpec(memory_space=pl.ANY)
HBM = pl.BlockSpec(memory_space=pltpu.HBM)
NT = (((1,), (1,)), ((), ()))
N_NEG = 32
Y_ORDER = (1, 3, 2)
QUERY_ROWS = 2
DIGIT = 64


def params(mib=40):
    return pltpu.CompilerParams(vmem_limit_bytes=mib * 1024 * 1024)


def cost(flops, size):
    return pl.CostEstimate(flops=flops, bytes_accessed=size, transcendentals=0)


def shift(block, axis, distance):
    n = lax.axis_size(axis)
    return lax.ppermute(block, axis, [(i, (i + distance) % n) for i in range(n)])


def cross(block, up):
    route = []
    for i in range(N_ZH):
        j = i if up else (i - 1) % N_ZH
        route += [(i, N_ZH + j), (N_ZH + j, i)]
    return lax.ppermute(block, ("grp", "zh"), route)


def reroute(block, target):
    route = []
    for g in range(N_GRP):
        for z in range(N_ZH):
            to_g, to_z = target(g, z)
            route.append((g * N_ZH + z, to_g * N_ZH + to_z % N_ZH))
    return lax.ppermute(block, ("grp", "zh"), route)


def at(axis):
    return lax.axis_index(axis)


def iota(shape, axis):
    return lax.broadcasted_iota(jnp.int32, shape, axis)


def onehot(hit):
    return jnp.where(hit, 1.0, 0.0).astype(BF)


def pack_kernel(w_in, w_out_t, packed, held, sems):
    shard = w_in.shape[0]
    n = packed.shape[0]
    copies = [
        pltpu.make_async_copy(w_in, held.at[0:shard], sems.at[n]),
        pltpu.make_async_copy(w_out_t, held.at[shard : 2 * shard], sems.at[n + 1]),
    ]
    for copy in copies:
        copy.start()
    for copy in copies:
        copy.wait()
    copies = [pltpu.make_async_copy(held, packed.at[z], sems.at[z]) for z in range(n)]
    for copy in copies:
        copy.start()
    for copy in copies:
        copy.wait()


def stage_kernel(x, b_in, x_out, b_out, sems):
    copies = [
        pltpu.make_async_copy(x, x_out, sems.at[0]),
        pltpu.make_async_copy(b_in, b_out, sems.at[1]),
    ]
    for copy in copies:
        copy.start()
    for copy in copies:
        copy.wait()


def slots():
    g, y, c = at("grp"), at("y"), at("c")
    found = []
    for other in range(N_C):
        core = c if other == 0 else 1 - c
        for far in range(N_GRP):
            group = g if far == 0 else 1 - g
            for k in (0,) + Y_ORDER:
                found.append((group, lax.rem(y - k + N_Y, N_Y) * N_C + core))
    return found


def ffn_kernel(x_ref, b_ref, *rest):
    sources = rest[:16]
    own_ref, s1, s2, s3 = rest[16:20]
    w, hidden, total, sems = rest[20:]
    m = at("mp")
    hid = hidden.shape[1]
    shard = w.shape[3] // 2
    copies = []
    for i, (group, slot) in enumerate(slots()):
        copies.append(pltpu.make_async_copy(sources[i], w.at[group, :, slot], sems.at[i]))
    for copy in copies:
        copy.start()
    for copy in copies:
        copy.wait()
    depth = x_ref.shape[1]
    tile = 256
    for t in range(hid // tile):
        cols = slice(t * tile, (t + 1) * tile)
        w_in = w[:, :, :, 0:shard, cols].reshape(depth, tile)
        pre = jnp.dot(x_ref[...], w_in, preferred_element_type=F32) + b_ref[:, cols]
        hidden[:, cols] = (0.5 * pre * (1.0 + lax.erf(pre * np.float32(0.5**0.5)))).astype(BF)
    planes = tile // (w.shape[2] * shard)
    per_group = w.shape[1] // planes
    for t in range(total.shape[1] // tile):
        begin = t % per_group * planes
        w_out = w[t // per_group, begin : begin + planes, :, shard:, :].reshape(tile, hid)
        total[:, t * tile : (t + 1) * tile] = lax.dot_general(
            hidden[...], w_out, NT, preferred_element_type=F32
        )
    rows = own_ref.shape[0]
    for k, out in ((2, s2), (1, s1), (3, s3), (0, own_ref)):
        j = lax.rem(m + k, N_MP)
        block = pl.ds(pl.multiple_of(j * rows, rows), rows)
        if k == 0:
            out[...] = total[block, :] + x_ref[block, :].astype(F32)
        else:
            out[...] = total[block, :].astype(BF)


def pieces(v):
    a = v.astype(BF)
    rest = v - a.astype(F32)
    b = rest.astype(BF)
    return a, b, (rest - b.astype(F32)).astype(BF)


def prep_kernel(b_out, gain, bias, lens, negs, counts, poss, vectors, live, count, lists_ref):
    m = at("mp")
    n_pass, rows = live.shape
    part = lists_ref.shape[1]
    vectors[0:1, :] = b_out[...]
    vectors[1:2, :] = gain[...]
    vectors[2:3, :] = bias[...]
    n_all = lens.shape[1]
    chosen = iota((n_pass, n_all), 1) == iota((n_pass, n_all), 0) + m * n_pass
    length = jnp.sum(jnp.where(chosen, lens[...].astype(F32), 0.0), axis=1, keepdims=True)
    row = iota((n_pass, rows), 1)
    slab = iota((n_pass, rows), 0)
    begin = ((row % WIN) * WINDOW_TOKENS).astype(F32)
    alive = jnp.where((row // WIN == slab) & (begin < length), 1.0, 0.0).astype(F32)
    live[...] = alive.astype(BF)
    count[...] = jnp.broadcast_to(jnp.sum(alive, axis=1, keepdims=True), count.shape)
    own_q, n_neg = negs.shape
    n_q = own_q // N_MP
    ids = negs[...]
    diag = iota((own_q, own_q), 0) == iota((own_q, own_q), 1)
    n_used = jnp.sum(jnp.where(diag, counts[...].astype(F32), 0.0), axis=1, keepdims=True)
    pos = jnp.sum(jnp.where(diag, poss[...].astype(F32), 0.0), axis=1, keepdims=True)
    pos = pos.astype(jnp.int32)
    wide = iota((n_neg, part), 1)
    deep = iota((n_neg, part), 0)
    high = (ids // DIGIT).astype(F32).astype(BF)
    low = (ids % DIGIT).astype(F32).astype(BF)
    lists = jnp.dot(high, onehot(wide == deep), preferred_element_type=F32)
    lists = lists + jnp.dot(low, onehot(wide == deep + n_neg), preferred_element_type=F32)
    lane = iota((own_q, part), 1)
    lists = jnp.where(lane == 2 * n_neg, n_used, lists)
    lists = jnp.where(lane == 2 * n_neg + 1, (pos // DIGIT).astype(F32), lists)
    lists = jnp.where(lane == 2 * n_neg + 2, (pos % DIGIT).astype(F32), lists)
    r8, c8 = iota((n_pass, own_q), 0), iota((n_pass, own_q), 1)
    move = onehot((r8 < n_q) & (c8 == m * n_q + r8))
    lists_ref[...] = jnp.dot(move, lists.astype(BF), preferred_element_type=F32).astype(BF)


def norm_kernel(own, r1, r2, r3, vectors, live, count, lists, p_ref, blocks):
    rows, width = own.shape
    summed = own[...] + r1[...].astype(F32) + r2[...].astype(F32) + r3[...].astype(F32)
    summed = summed + vectors[0:1, :]
    center = jnp.mean(summed, axis=1, keepdims=True)
    off = summed - center
    spread_ = jnp.mean(off * off, axis=1, keepdims=True)
    coded = (off * lax.rsqrt(spread_ + EPS_NORM) * vectors[1:2, :] + vectors[2:3, :]).astype(BF)

    n_pass = p_ref.shape[0]
    p = (jnp.dot(live[...], coded, preferred_element_type=F32) / count[:, 0:1]).astype(BF)
    n_pass = p_ref.shape[0]
    pf = p.astype(F32)
    square = pieces(jnp.sum(pf * pf, axis=1, keepdims=True))
    lane = iota((n_pass, 128), 1)
    tail = jnp.zeros((n_pass, 128), F32)
    for i, piece in enumerate(square):
        tail = jnp.where(lane == i, piece.astype(F32), tail)
    n_pass = p_ref.shape[0]
    pick = onehot(iota((n_pass, rows), 1) // QLEN == iota((n_pass, rows), 0))
    q = (jnp.dot(pick, coded, preferred_element_type=F32) * (1.0 / QLEN)).astype(BF)
    refresh = at("grp") == 1
    p_ref[:, :width] = jnp.where(refresh, p, q)
    p_ref[:, width:] = jnp.where(refresh, tail.astype(BF), lists[...])
    part = width // N_MP
    for j in range(N_MP):
        blocks[j, :rows, :] = coded[:, j * part : (j + 1) * part]
        blocks[j, rows:, :] = jnp.zeros((16, part), BF)


def send_kernel(blocks, mine, came, send, held, sems):
    part = held.shape[1]
    rows = send.shape[1] - 16
    width = part * N_MP
    n_q = rows // QLEN
    rider = jnp.where(at("grp") == 1, came[0:16, :], mine[0:16, :])
    parts = [rider[:, j * part : (j + 1) * part] for j in range(N_MP)]
    lists = jnp.concatenate([rider[:, width:], rider[:, width:]], axis=1)
    stacked = jnp.concatenate(parts + [lists], axis=0)
    shape = (16, 16 * (N_MP + 1))
    to, come = iota(shape, 0), iota(shape, 1)
    move = onehot((to == come // 16 * n_q + come % 16) & (come % 16 < n_q))
    held[...] = jnp.dot(move, stacked, preferred_element_type=F32).astype(BF)
    copies = [
        pltpu.make_async_copy(held, send.at[j, rows : rows + 16], sems.at[j]) for j in range(N_MP)
    ]
    for copy in copies:
        copy.start()
    for copy in copies:
        copy.wait()


def query_kernel(arrived, q_ref, lists):
    part = arrived.shape[2]
    held = arrived[0:N_MP, arrived.shape[1] - 16 :, :].reshape(N_MP * 16, part)
    own = QUERY_ROWS
    shape = ((N_MP + 1) * 16, N_MP * 16)
    r, col = iota(shape, 0), iota(shape, 1)
    chunk, row = r // 16, r % 16
    take = onehot((col // 16 == row // own) & (col % 16 == chunk * own + row % own))
    got = jnp.dot(take, held, preferred_element_type=F32)
    for j in range(N_MP):
        q_ref[:, j * part : (j + 1) * part] = got[16 * j : 16 * (j + 1)].astype(BF)
    lists[...] = got[16 * N_MP :]


def unpack_kernel(arrived, encoded):
    rows = encoded.shape[0] // N_MP
    for j in range(N_MP):
        encoded[j * rows : (j + 1) * rows, :] = arrived[j, 0:rows, :]


def score_kernel(q_ref, lists_ref, *rest):
    blocks, out = rest[:-1], rest[-1]
    g, zh, y, c, m = at("grp"), at("zh"), at("y"), at("c"), at("mp")
    size = blocks[0].shape[0]
    each = size // N_GRP
    width = q_ref.shape[1]
    part = width // N_MP
    n_q = out.shape[1] // 2
    q = q_ref[...]
    qf = q.astype(F32)
    a = jnp.sqrt(jnp.sum(qf * qf, axis=1, keepdims=True) / width + EPS_UNIT)[:n_q]
    lists = lists_ref[:n_q, :]
    neg = lists[:, :N_NEG] * DIGIT + lists[:, N_NEG : 2 * N_NEG]
    count = lists[:, 2 * N_NEG : 2 * N_NEG + 1]
    pos = lists[:, 2 * N_NEG + 1 : 2 * N_NEG + 2] * DIGIT + lists[:, 2 * N_NEG + 2 : 2 * N_NEG + 3]
    slot = iota(neg.shape, 1).astype(F32)
    neg = jnp.where(slot < count, neg, -1.0)
    dots, squares = [], []
    first_three = onehot(iota((16, 128), 1) < 3)
    for block in blocks:
        dots.append(
            lax.dot_general(q, block[:, :width], NT, preferred_element_type=F32)[:n_q]
        )
        squares.append(
            lax.dot_general(first_three, block[:, width:], NT, preferred_element_type=F32)[:1]
        )
    dots = jnp.concatenate(dots, axis=1)
    b = jnp.sqrt(jnp.concatenate(squares, axis=1) / width + EPS_UNIT)
    n_p = dots.shape[1]
    s = dots / (width * SHARPNESS * a * b)
    lane = iota((1, n_p), 1)
    per_core = size * N_Y
    core = lax.rem(c + lane // per_core, N_C)
    turn = lax.rem(lane, per_core) // size
    turn = jnp.where(turn < 2, turn, 5 - turn)
    line = lax.rem(y - turn + N_Y, N_Y)
    piece = lax.rem(lane, size) // each
    slab = lax.rem(zh + g * piece + (1 - g) * (N_ZH - 1) * (1 + piece), N_ZH)
    number = ((slab * N_Y + line) * N_C + core) * (each * N_MP) + m * each + lax.rem(lane, each)
    number = number.astype(F32)
    match = jnp.where(pos == number, 1.0, 0.0).astype(F32)
    cand = jnp.zeros((n_q, n_p), F32)
    for j in range(N_NEG):
        cand = cand + jnp.where(neg[:, j : j + 1] == number, 1.0, 0.0)
    w = jnp.exp(s) * cand
    total = jnp.sum(w, axis=1, keepdims=True)
    score_pos = jnp.sum(s * match, axis=1, keepdims=True)
    unit = 1.0 / (np.float32(width**0.5) * b)
    coef = jnp.concatenate(pieces(w * unit) + pieces(match * unit), axis=0)
    grads = jnp.zeros((6 * n_q, width), F32)
    for i, block in enumerate(blocks):
        grads = grads + jnp.dot(
            coef[:, i * size : (i + 1) * size], block[:, :width], preferred_element_type=F32
        )
    pull = grads[:n_q] + grads[n_q : 2 * n_q] + grads[2 * n_q : 3 * n_q]
    toward = grads[3 * n_q : 4 * n_q] + grads[4 * n_q : 5 * n_q] + grads[5 * n_q :]
    stats = jnp.where(iota((n_q, 128), 1) < 64, total, score_pos)
    for g in range(N_GRP):
        for mm in range(N_MP):
            cols = slice(mm * part, (mm + 1) * part)
            d = g * N_MP + mm
            out[d, 0:n_q, 0:part] = pull[:, cols]
            out[d, n_q:, 0:part] = toward[:, cols]
            out[d, 0:n_q, part:] = stats
            out[d, n_q:, part:] = stats


def final_kernel(arrived, grad, loss):
    own, part = grad.shape
    acc = arrived[0]
    for d in range(1, arrived.shape[0]):
        acc = acc + arrived[d]
    others = acc[:own, part : part + 1]
    score = acc[:own, part + 64 : part + 65]
    total = others + jnp.exp(score)
    pull, toward = acc[:own, :part], acc[own:, :part]
    grad[...] = (pull / total - toward * (others / total)) / SHARPNESS
    column = jnp.log(total) - score
    diagonal = iota((own, 128), 0) == iota((own, 128), 1)
    row = jnp.sum(jnp.where(diagonal, column, 0.0), axis=0, keepdims=True)
    loss[...] = row[:, :own]


def body(states, w_in, b_in, w_out, b_out, ln_gain, ln_bias, lengths, neg_ids, neg_count, pos_ids):
    x = states[0]
    rows, width = x.shape
    hid = b_in.shape[0]
    shard = w_in.shape[0]
    part_rows = rows // N_MP
    part = width // N_MP
    n_pass = part_rows // WIN
    own_q = part_rows // QLEN * N_MP
    peers = N_GRP * N_MP
    shape = jax.ShapeDtypeStruct

    packed = pl.pallas_call(
        pack_kernel,
        out_shape=shape((N_ZH, 2 * shard, hid), BF),
        in_specs=[HBM] * 2,
        out_specs=VMEM,
        scratch_shapes=[
            pltpu.VMEM((2 * shard, hid), BF),
            pltpu.SemaphoreType.DMA((N_ZH + 2,)),
        ],
        compiler_params=params(60),
        name="pack",
    )(w_in, w_out.T)
    lines = [lax.all_to_all(packed, "zh", 0, 0, tiled=True)]
    x, b_in = pl.pallas_call(
        stage_kernel,
        out_shape=[shape((rows, width), BF), shape((1, hid), F32)],
        in_specs=[HBM] * 2,
        out_specs=[VMEM] * 2,
        scratch_shapes=[pltpu.SemaphoreType.DMA((2,))],
        compiler_params=params(20),
        name="stage",
    )(x, b_in[None])
    lines[0], x, b_in = lax.optimization_barrier((lines[0], x, b_in))
    far = [cross(lines[0], True)]
    for k in Y_ORDER:
        lines.append(shift(lines[0], "y", k))
    far = far + [cross(lines[i], Y_ORDER[i - 1] == 2) for i in (1, 2, 3)]
    lines = lines + far
    lines = lines + [shift(v, "c", 1) for v in lines]
    weights = pltpu.VMEM((N_GRP, N_ZH, N_Y * N_C, 2 * shard, hid), BF)
    own, s1, s2, s3 = pl.pallas_call(
        ffn_kernel,
        out_shape=[shape((part_rows, width), F32)] + [shape((part_rows, width), BF)] * 3,
        in_specs=[VMEM] * 2 + [ANY] * 16,
        out_specs=[VMEM] * 4,
        scratch_shapes=[
            weights,
            pltpu.VMEM((rows, hid), BF),
            pltpu.VMEM((rows, width), F32),
            pltpu.SemaphoreType.DMA((16,)),
        ],
        compiler_params=params(20),
        cost_estimate=cost(4 * rows * width * hid, 8 << 20),
        name="ffn",
    )(x, b_in, *lines)
    r1, r3, r2 = shift(s1, "mp", 1), shift(s3, "mp", 3), shift(s2, "mp", 2)
    small = [
        b_out[None],
        ln_gain[None],
        ln_bias[None],
        lengths[None],
        neg_ids,
        neg_count[None],
        pos_ids[None],
    ]
    r1, *small = lax.optimization_barrier((r1, *small))
    vectors, live, count, lists = pl.pallas_call(
        prep_kernel,
        out_shape=[
            shape((3, width), F32),
            shape((n_pass, part_rows), BF),
            shape((n_pass, 128), F32),
            shape((n_pass, 128), BF),
        ],
        in_specs=[VMEM] * 7,
        out_specs=[VMEM] * 4,
        compiler_params=params(),
        name="prep",
    )(*small)

    passages, blocks = pl.pallas_call(
        norm_kernel,
        out_shape=[
            shape((n_pass, width + 128), BF),
            shape((N_MP, part_rows + 16, part), BF),
        ],
        in_specs=[VMEM] * 8,
        out_specs=[VMEM] * 2,
        compiler_params=params(),
        cost_estimate=cost(2 * part_rows * width * 64, 3 << 20),
        name="norm",
    )(own, r1, r3, r2, vectors, live, count, lists)

    near = reroute(passages, lambda g, z: (1 - g, z + 1 if g else z))
    mid = reroute(passages, lambda g, z: (g, z - 1))
    far = reroute(passages, lambda g, z: (1 - g, z - 2 if g else z + 2))
    refresh = at("grp") == 1
    slab = jnp.concatenate(
        [jnp.where(refresh, passages, near), jnp.where(refresh, mid, far)], axis=0
    )
    lines = [slab] + [shift(slab, "y", k) for k in Y_ORDER]
    send = pl.pallas_call(
        send_kernel,
        out_shape=shape(blocks.shape, BF),
        in_specs=[ANY, VMEM, VMEM],
        out_specs=ANY,
        scratch_shapes=[pltpu.VMEM((16, part), BF), pltpu.SemaphoreType.DMA((N_MP,))],
        input_output_aliases={0: 0},
        compiler_params=params(),
        name="send",
    )(blocks, passages, near)
    arrived = lax.all_to_all(send, "mp", 0, 0, tiled=True)
    q_all, lists = pl.pallas_call(
        query_kernel,
        out_shape=[shape((16, width), BF), shape((16, part), F32)],
        in_specs=[VMEM],
        out_specs=[VMEM] * 2,
        compiler_params=params(),
        name="query",
    )(arrived)
    encoded = pl.pallas_call(
        unpack_kernel,
        out_shape=shape((rows, part), BF),
        in_specs=[VMEM],
        out_specs=VMEM,
        compiler_params=params(),
        name="unpack",
    )(arrived)
    lines[3], q_all = lax.optimization_barrier((lines[3], q_all))
    lines[2], encoded = lax.optimization_barrier((lines[2], encoded))
    lines = lines + [shift(v, "c", 1) for v in lines]
    shares = pl.pallas_call(
        score_kernel,
        out_shape=shape((peers, 2 * own_q, part + 128), F32),
        in_specs=[VMEM] * 10,
        out_specs=VMEM,
        compiler_params=params(),
        cost_estimate=cost(2 * 512 * width * 100, 3 << 20),
        name="score",
    )(q_all, lists, *lines)
    arrived = lax.all_to_all(shares, ("grp", "mp"), 0, 0, tiled=True)
    grad, loss = pl.pallas_call(
        final_kernel,
        out_shape=[shape((own_q, part), F32), shape((1, own_q), F32)],
        in_specs=[VMEM],
        out_specs=[VMEM] * 2,
        compiler_params=params(),
        name="final",
    )(arrived)
    return encoded[None], grad, loss.reshape(own_q)


def solution(mesh):
    fine = Mesh(
        mesh.devices.reshape(N_GRP, N_ZH, N_Y, N_C, N_MP), ("grp", "zh", "y", "c", "mp")
    )
    dp = ("zh", "y", "c")
    placed = (
        P("grp", dp, None),
        P(("grp",) + dp, "mp"),
        P("mp"),
        P("mp", ("grp",) + dp),
        P(),
        P(),
        P(),
        P(dp),
        P(dp, None),
        P(dp),
        P(dp),
    )
    return jax.shard_map(
        body,
        mesh=fine,
        in_specs=placed,
        out_specs=(P("grp", dp, "mp"), P(dp, "mp"), P(dp)),
        check_vma=False,
    )
```
